128 devices in a mesh: row: 4 (over y_hi, core), col: 32 (over z, y_lo, x).
Axes of the slice: x: 4, y: 4 (y_hi: 2, y_lo: 2; y = y_hi * 2 + y_lo), z: 4, core: 2. Of those that a mesh axis runs over, the one named last changes fastest.
Arguments:
- activations: bfloat16 [4096, 8192], P('row', 'col'), may hold values from -90 to 90
- norm_gain: bfloat16 [8192], P('col'), may hold values from 0.099609375 to 1.8984375
- w_query: bfloat16 [8192, 8192], P('row', 'col'), may hold values from -0.26516504 to 0.26516504
- w_key: bfloat16 [8192, 1024], P('row'), may hold values from -0.044194174 to 0.044194174
- w_value: bfloat16 [8192, 1024], P('row'), may hold values from -0.0625 to 0.0625
- w_out: bfloat16 [8192, 8192], P('row', 'col'), may hold values from -0.0625 to 0.0625
Outputs:
- output: bfloat16 [4096, 8192], P('row', 'col')
The draws below stay inside these ranges and needn't reach their ends.
All inputs are finite; a program needn't handle non-finite values.
Results may differ from the reference program's by a relative error of at most 0.018.
Values may be sent and summed in bfloat16 or wider, within the bound.
A program may use at most 128 MiB of HBM per device.

```python
import jax
import jax.numpy as jnp
from jax import lax

D = 8192
HEADS = 64
KV_HEADS = 8
HEAD_DIM = 128
LENGTH = 4096
Q_COLS = 8192
KV_COLS = 1024


def shared_keys(key):
    base_draw = jax.random.normal(jax.random.fold_in(key, 101), (D, KV_HEADS * HEAD_DIM), jnp.float32)
    return jnp.clip(base_draw, -3.96, 3.96) * D ** (-0.5)


def draw_w_key(key, part):
    key_block = shared_keys(key)
    return key_block.astype(jnp.bfloat16)


def draw_w_query(key, part):
    key = jax.random.fold_in(key, 2)
    private_part = jnp.clip(jax.random.normal(key, (D, HEADS * HEAD_DIM), jnp.float32), -4.0, 4.0) * D ** (-0.5)
    return private_part.astype(jnp.bfloat16)


def draw_activations(key, part):
    key = jax.random.fold_in(key, 3)
    column_draw = jax.random.uniform(jax.random.fold_in(key, 1), (D,), jnp.float32, -0.5, 0.5)
    row_draw = jax.random.uniform(jax.random.fold_in(key, 2), (LENGTH, 1), jnp.float32, -0.5, 0.5)
    feature_pos = jnp.arange(D, dtype=jnp.float32) / D
    column_scale = jnp.sqrt(3.0) ** feature_pos * 10.0 ** column_draw
    noise_part = jnp.clip(jax.random.normal(jax.random.fold_in(key, 4), (LENGTH, D), jnp.float32), -4.0, 4.0)
    row_scale = 10.0 ** row_draw
    return (noise_part * column_scale[None, :] * row_scale).astype(jnp.bfloat16)


def level_of(rng, extent, split, smallest, high):
    loudness = 1.0
    for axis_at, shards_of in split:
        draws = jax.random.uniform(jax.random.fold_in(jax.random.fold_in(rng, 6), axis_at), (shards_of,), jnp.float32, smallest / len(split), high / len(split))
        loudness = loudness * jnp.repeat(jnp.exp(draws), extent[axis_at] // shards_of).reshape((-1,) + (1,) * (len(extent) - 1 - axis_at))
    return loudness


def normal_values(rng, shape, width, reach, pieces=(), kind=jnp.bfloat16):
    result = jax.random.normal(rng, shape, jnp.float32) * width
    if len(pieces) > 0:
        result = level_of(rng, shape, pieces, -0.22, 0.18) * result
    return jnp.clip(result, min=-reach, max=reach).astype(kind)


def setup_inputs(seed: int = 0) -> dict:
    seeds = jax.random.split(jax.random.key(seed), 7)
    activations = draw_activations(jax.random.fold_in(seeds[6], 71), 0)
    norm_gain = jnp.clip(1.0 + 0.18 * jax.random.normal(seeds[1], (D,), jnp.float32), 0.099609375, 1.8984375).astype(jnp.bfloat16)
    w_query = draw_w_query(jax.random.fold_in(seeds[6], 71), 0)
    w_key = draw_w_key(jax.random.fold_in(seeds[6], 71), 0)
    w_value = normal_values(seeds[4], (D, KV_COLS), D ** -0.5, 0.0625, ((0, 4),))
    w_out = normal_values(seeds[5], (Q_COLS, D), Q_COLS ** -0.5, 0.0625, ((0, 4), (1, 32)))
    return dict(activations=activations, norm_gain=norm_gain, w_query=w_query, w_key=w_key, w_value=w_value, w_out=w_out)


def rope_tables(count, offset, head_size):
    half_size = head_size // 2
    exponent = jnp.arange(half_size, dtype=jnp.float32) * (2.0 / head_size)
    frequency = jnp.exp(-jnp.log(500000.0) * exponent)
    position = (offset + jnp.arange(count, dtype=jnp.int32)).astype(jnp.float32)
    angles = position[:, None] * frequency[None, :]
    return (jnp.cos(angles), jnp.sin(angles))

def rotate(stacked, cos_table, sin_table):
    half_size = stacked.shape[-1] // 2
    leading = stacked[..., :half_size]
    trailing = stacked[..., half_size:]
    cosine = cos_table[:, None, :]
    sine_part = sin_table[:, None, :]
    return jnp.concatenate([leading * cosine - trailing * sine_part, trailing * cosine + leading * sine_part], axis=-1)

def reference(activations, norm_gain, w_query, w_key, w_value, w_out):
    values_wide = activations.astype(jnp.float32)
    inverse_rms = lax.rsqrt(lax.optimization_barrier(jnp.mean(values_wide * values_wide, axis=1)) + 1e-05)
    hidden = (values_wide * inverse_rms[:, None] * norm_gain.astype(jnp.float32)[None, :]).astype(jnp.bfloat16)
    query = jnp.dot(hidden, w_query, preferred_element_type=jnp.float32)
    key_part = jnp.dot(hidden, w_key, preferred_element_type=jnp.float32).astype(jnp.bfloat16)
    value_part = jnp.dot(hidden, w_value, preferred_element_type=jnp.float32).astype(jnp.bfloat16)
    cos_table, sin_table = rope_tables(LENGTH, 0, HEAD_DIM)
    query_rot = rotate(query.reshape(LENGTH, HEADS, HEAD_DIM), cos_table, sin_table).astype(jnp.bfloat16)
    key_rot = rotate(key_part.astype(jnp.float32).reshape(LENGTH, KV_HEADS, HEAD_DIM), cos_table, sin_table).astype(jnp.bfloat16)
    value_heads = value_part.reshape(LENGTH, KV_HEADS, HEAD_DIM)
    position = jnp.arange(LENGTH, dtype=jnp.int32)
    allowed = position[None, :] <= position[:, None]
    group_size = HEADS // KV_HEADS

    def one_head(head_index):
        query_head = lax.dynamic_index_in_dim(query_rot, head_index, 1, keepdims=False)
        kv_index = head_index // group_size
        key_head = lax.dynamic_index_in_dim(key_rot, kv_index, 1, keepdims=False)
        value_head = lax.dynamic_index_in_dim(value_heads, kv_index, 1, keepdims=False)
        scores = jnp.dot(query_head, key_head.T, preferred_element_type=jnp.float32) * HEAD_DIM ** (-0.5)
        masked = jnp.where(allowed, scores, -1e+30)
        row_max = lax.optimization_barrier(jnp.max(masked, axis=1, keepdims=True))
        exponentials = jnp.where(allowed, jnp.exp(masked - row_max), 0.0)
        denominators = lax.optimization_barrier(jnp.sum(exponentials, axis=1))
        mixed = jnp.dot(exponentials.astype(jnp.bfloat16), value_head, preferred_element_type=jnp.float32)
        return (mixed / denominators[:, None]).astype(jnp.bfloat16)
    per_head = lax.map(one_head, jnp.arange(HEADS, dtype=jnp.int32))
    attended = jnp.transpose(per_head, (1, 0, 2)).reshape(LENGTH, HEADS * HEAD_DIM)
    return jnp.dot(attended, w_out, preferred_element_type=jnp.float32).astype(jnp.bfloat16)
```

```python
import functools

import jax
import jax.numpy as jnp
import numpy as np
from jax import lax
from jax.experimental import pallas as pl
from jax.experimental.pallas import tpu as pltpu
from jax.sharding import PartitionSpec as P

MESH = pl.DeviceIdType.MESH
HEAD_DIM = 128
TOK = 1024
B = 256
CHUNKS = TOK // B
LENGTH = 4096
D = 8192
SCALE = HEAD_DIM**-0.5 * 1.4426950408889634
F32 = jnp.float32
BF16 = jnp.bfloat16


def rope_constants():
    half = HEAD_DIM // 2
    frequency = np.exp(-np.log(500000.0) * (np.arange(half) * (2.0 / HEAD_DIM)))
    angles = np.arange(LENGTH)[:, None] * frequency[None, :]
    cos, sin = np.cos(angles), np.sin(angles)
    return (
        np.concatenate([cos, cos], 1).astype(np.float32),
        np.concatenate([-sin, sin], 1).astype(np.float32),
    )


def remote(src, dst, send, recv, device):
    return pltpu.make_async_remote_copy(
        src_ref=src, dst_ref=dst, send_sem=send, recv_sem=recv, device_id=device, device_id_type=MESH
    )


def block(i, size=B):
    return pl.ds(pl.multiple_of(i * size, size), size)


def kernel(
    act, gain, wq, wk, wv, wo, cos_all, sin_all, out,
    a1, a2, w, wkv, wout, stage1, stage2, got1, got2, own1, own2, kv_stage, kv_got, kv_own, kvo, inv, cos, sin, q,
    ss1, ss2,
    loc_sem, ag_s, ag_r, ss_s, ss_r, ssx_s, ssx_r, w_s, w_r, wf_s, wf_r, kvw_s, kvw_r, rs_s, rs_r, kvp_s, kvp_r, kvg_s,
    kvg_r, kvf_s, kvf_r,
):
    row, col = lax.axis_index("row"), lax.axis_index("col")
    yh, co = row // 2, row % 2
    z, yl, x = col // 8, (col // 4) % 2, col % 4
    g = z * 2 + yl

    def at(yh_, co_, z_, yl_, x_):
        return (yh_ * 2 + co_, z_ * 8 + yl_ * 4 + x_)

    z_peers = [at(yh, co, (z + d) % 4, yl, x) for d in (1, 3, 2)]
    yl_peer = at(yh, co, z, 1 - yl, x)
    x_at = [(x + d) % 4 for d in (1, 3, 2)]
    x_peers = [at(yh, co, z, yl, v) for v in x_at]
    far_at = [(x + d) % 4 for d in (2, 1, 3, 0)]
    far_peers = [at(1 - yh, co, z, yl, v) for v in far_at]
    y_peer = at(1 - yh, co, z, yl, x)
    sibling = at(yh, 1 - co, z, yl, x)

    barrier = pltpu.get_barrier_semaphore()
    everyone = z_peers + [yl_peer] + x_peers + far_peers + [sibling]
    for peer in everyone:
        pl.semaphore_signal(barrier, inc=1, device_id=peer, device_id_type=MESH)

    sent = []

    def send(src, dst, s, r, device):
        copy = remote(src, dst, s, r, device)
        copy.start()
        sent.append(copy)

    def arrived(dst, s, r):
        remote(dst, dst, s, r, sibling).wait_recv()

    local = [
        pltpu.make_async_copy(cos_all.at[block(row, TOK)], cos, loc_sem.at[0]),
        pltpu.make_async_copy(sin_all.at[block(row, TOK)], sin, loc_sem.at[1]),
        pltpu.make_async_copy(wk.at[:, x, :, block(g, 128)], wkv.at[pl.ds(2 * row, 2), :, pl.ds(0, 128)], loc_sem.at[2]),
        pltpu.make_async_copy(wv.at[:, x, :, block(g, 128)], wkv.at[pl.ds(2 * row, 2), :, pl.ds(128, 128)], loc_sem.at[3]),
        pltpu.make_async_copy(wq.at[:, x], w.at[pl.ds(2 * row, 2), :, block(x)], loc_sem.at[4]),
        pltpu.make_async_copy(wo.at[:, x], wout.at[pl.ds(2 * row, 2), :, block(x)], loc_sem.at[5]),
    ]
    for copy in local:
        copy.start()
    wide = act[...].astype(F32)
    a1[:, block(g)] = (wide * gain[...].astype(F32)).astype(BF16)
    square = wide * wide
    high = square.astype(BF16)
    low = (square - high.astype(F32)).astype(BF16)
    ones = jnp.ones((8, B), BF16)
    along = (((1,), (1,)), ((), ()))
    sums = lax.dot_general(ones, high, along, preferred_element_type=F32) + lax.dot_general(
        ones, low, along, preferred_element_type=F32
    )
    ss1[g] = sums[0:1]
    kvo[:, 2 * HEAD_DIM :] = jnp.ones((LENGTH, HEAD_DIM), BF16)

    pl.semaphore_wait(barrier, len(everyone))

    def kv_slab(r):
        return wkv.at[pl.ds(2 * r, 2)]

    local[2].wait()
    local[3].wait()
    send(kv_slab(row), kv_slab(row), kvw_s.at[0], kvw_r.at[0], y_peer)
    send(kv_slab(row), kv_slab(row), kvw_s.at[1], kvw_r.at[1], sibling)

    def gather_send(phase, a, t):
        tile = a.at[pl.ds(t * B, B), block(g)]
        for k, peer in enumerate([yl_peer] + z_peers):
            send(tile, tile, ag_s.at[phase, t, k], ag_r.at[phase, t, g], peer)

    def gather_pass(phase, a, t):
        other = z * 2 + 1 - yl
        tile = a.at[pl.ds(t * B, B), block(other)]
        arrived(tile, ag_s.at[phase, t, 0], ag_r.at[phase, t, other])
        for k, peer in enumerate(z_peers):
            send(tile, tile, ag_s.at[phase, t, 4 + k], ag_r.at[phase, t, other], peer)

    def gather_wait(phase, a, t):
        for d in (1, 3, 2):
            for yl_ in range(2):
                who = ((z + d) % 4) * 2 + yl_
                arrived(a.at[pl.ds(t * B, B), block(who)], ag_s.at[phase, t, 0], ag_r.at[phase, t, who])

    def weight_send(phase, src, dst):
        piece = dst.at[pl.ds(2 * row, 2), :, block(x)]
        for k, (xd, peer) in enumerate(zip(far_at, far_peers)):
            send(src.at[:, xd], piece, w_s.at[phase, k], w_r.at[phase, 1, x], peer)
        for k, (xd, peer) in enumerate(zip(x_at, x_peers)):
            send(src.at[:, xd], piece, w_s.at[phase, 4 + k], w_r.at[phase, 0, x], peer)

    far_row = (1 - yh) * 2 + co

    def weight_pass(phase, dst):
        for xs in x_at:
            arrived(dst.at[pl.ds(2 * row, 2), :, block(xs)], w_s.at[phase, 0], w_r.at[phase, 0, xs])
        local[4 + phase].wait()
        slab = dst.at[pl.ds(2 * row, 2)]
        send(slab, slab, wf_s.at[phase, 0], wf_r.at[phase, 0], sibling)
        for xs in far_at:
            arrived(dst.at[pl.ds(2 * far_row, 2), :, block(xs)], w_s.at[phase, 0], w_r.at[phase, 1, xs])
        slab = dst.at[pl.ds(2 * far_row, 2)]
        send(slab, slab, wf_s.at[phase, 1], wf_r.at[phase, 1], sibling)

    def weight_wait(phase, dst):
        arrived(dst.at[pl.ds(2 * (row + 1 - 2 * co), 2)], wf_s.at[phase, 0], wf_r.at[phase, 0])
        arrived(dst.at[pl.ds(2 * (far_row + 1 - 2 * co), 2)], wf_s.at[phase, 1], wf_r.at[phase, 1])

    def partial_send(phase, a, weights, stage, got, own, t):
        rows = pl.ds(t * B, B)
        for k, (xd, peer) in enumerate(zip(x_at, x_peers)):
            part = jnp.dot(
                a[rows, :], weights[:, :, block(xd)].reshape(8 * B, B), preferred_element_type=F32
            )
            stage[k, rows, :] = part.astype(BF16)
            send(stage.at[k, rows], got.at[x, rows], rs_s.at[phase, t, k], rs_r.at[phase, t, x], peer)
        own[rows, :] = jnp.dot(a[rows, :], weights[:, :, block(x)].reshape(8 * B, B), preferred_element_type=F32)

    def partial_sum(phase, got, own, t):
        rows = pl.ds(t * B, B)
        total = own[rows, :]
        for xs in x_at:
            arrived(got.at[xs, rows], rs_s.at[phase, t, 0], rs_r.at[phase, t, xs])
            total = total + got[xs, rows, :].astype(F32)
        return total

    for k, peer in enumerate([yl_peer] + z_peers):
        send(ss1.at[g], ss1.at[g], ss_s.at[k], ss_r.at[g], peer)
    for t in range(CHUNKS):
        gather_send(0, a1, t)
        if t == 0:
            weight_send(0, wq, w)

    arrived(kv_slab(far_row), kvw_s.at[0], kvw_r.at[0])
    send(kv_slab(far_row), kv_slab(far_row), kvw_s.at[2], kvw_r.at[2], sibling)
    arrived(kv_slab(row + 1 - 2 * co), kvw_s.at[1], kvw_r.at[1])

    other = z * 2 + 1 - yl
    arrived(ss1.at[other], ss_s.at[0], ss_r.at[other])
    for k, peer in enumerate(z_peers):
        send(ss1.at[other], ss1.at[other], ss_s.at[4 + k], ss_r.at[other], peer)

    arrived(kv_slab(far_row + 1 - 2 * co), kvw_s.at[2], kvw_r.at[2])

    def kv_copy(t):
        rows = pl.ds(t * B, B)
        return remote(kv_stage.at[rows], kv_got.at[x], kvp_s.at[t], kvp_r.at[x], at(yh, co, z, yl, t))

    def kv_part(t):
        rows = pl.ds(t * B, B)
        part = jnp.dot(a1[rows, :], wkv[...].reshape(8 * B, B), preferred_element_type=F32)
        kv_stage[rows, :] = part.astype(BF16)

        @pl.when(x != t)
        def _():
            kv_copy(t).start()

        @pl.when(x == t)
        def _():
            kv_own[...] = part

    for t in range(CHUNKS):
        gather_pass(0, a1, t)
        gather_wait(0, a1, t)
        kv_part(t)
        if t == 0:
            for d in (1, 3, 2):
                for yl_ in range(2):
                    who = ((z + d) % 4) * 2 + yl_
                    arrived(ss1.at[who], ss_s.at[0], ss_r.at[who])
            ss2[x] = jnp.sum(ss1[...], axis=0)
            for k, peer in enumerate(x_peers):
                send(ss2.at[x], ss2.at[x], ssx_s.at[k], ssx_r.at[x], peer)

    weight_pass(0, w)
    weight_wait(0, w)
    for t in range(CHUNKS):
        partial_send(0, a1, w, stage1, got1, own1, t)
    weight_send(1, wo, wout)

    for xs in x_at:
        arrived(ss2.at[xs], ssx_s.at[0], ssx_r.at[xs])
    factor = lax.rsqrt(jnp.sum(ss2[...], axis=0) / D + 1e-05)
    for b in range(TOK // 128):
        inv[pl.ds(b * 128, 128), :] = jnp.broadcast_to(factor[:, b * 128 : (b + 1) * 128], (128, 128)).T
    local[0].wait()
    local[1].wait()

    mine = block(x)
    total = kv_own[...]
    for xs in x_at:
        arrived(kv_got.at[xs], kvp_s.at[0], kvp_r.at[xs])
        total = total + kv_got[xs].astype(F32)
    scale = inv[mine, :]
    key = total[:, :HEAD_DIM] * scale
    key = (key * cos[mine, :] + pltpu.roll(key, HEAD_DIM // 2, 1) * sin[mine, :]).astype(BF16)
    value = (total[:, HEAD_DIM:] * scale).astype(BF16)
    kvo[block(row * 4 + x), 0 : 2 * HEAD_DIM] = jnp.concatenate([key, value], axis=1)

    def quarter(r, xs):
        return kvo.at[block(r * 4 + xs), pl.ds(0, 2 * HEAD_DIM)]

    def whole(r):
        return kvo.at[block(r, TOK), pl.ds(0, 2 * HEAD_DIM)]

    def kv_down():
        return remote(quarter(row, x), quarter(row, x), kvg_s.at[3], kvg_r.at[row, x], y_peer)

    def kv_across(which, r):
        return remote(whole(r), whole(r), kvf_s.at[which], kvf_r.at[which], sibling)

    @pl.when(yh == 0)
    def _():
        kv_down().start()

    for k, peer in enumerate(x_peers):
        send(quarter(row, x), quarter(row, x), kvg_s.at[k], kvg_r.at[row, x], peer)

    above = row - 2

    def kv_relay():
        return [
            remote(quarter(above, x), quarter(above, x), kvg_s.at[4 + k], kvg_r.at[above, x], peer)
            for k, peer in enumerate(x_peers)
        ]

    @pl.when(yh == 1)
    def _():
        arrived(quarter(above, x), kvg_s.at[0], kvg_r.at[above, x])
        for copy in kv_relay():
            copy.start()

    for xs in x_at:
        arrived(quarter(row, xs), kvg_s.at[0], kvg_r.at[row, xs])

    @pl.when(co == 0)
    def _():
        kv_across(0, row).start()

    @pl.when(yh == 1)
    def _():
        for xs in x_at:
            arrived(quarter(above, xs), kvg_s.at[0], kvg_r.at[above, xs])
        kv_across(1, above).start()
        arrived(whole(above + 1 - 2 * co), kvf_s.at[1], kvf_r.at[1])

    @pl.when(co == 1)
    def _():
        arrived(whole(row - 1), kvf_s.at[0], kvf_r.at[0])

    for t in range(CHUNKS):
        rows = pl.ds(t * B, B)
        total = partial_sum(0, got1, own1, t)
        scale = inv[rows, :] * SCALE
        for h in range(2):
            part = total[:, h * HEAD_DIM : (h + 1) * HEAD_DIM] * scale
            part = part * cos[rows, :] + pltpu.roll(part, HEAD_DIM // 2, 1) * sin[rows, :]
            q[pl.ds(h * B, B), :] = part.astype(BF16)
        width = (t + 1) * B
        here = kvo[pl.ds(pl.multiple_of(row * TOK, TOK), width), :]
        queries = q[...]
        s = lax.dot_general(queries, here[:, :HEAD_DIM], along, preferred_element_type=F32)
        query_at = lax.broadcasted_iota(jnp.int32, s.shape, 0) % B + t * B
        key_at = lax.broadcasted_iota(jnp.int32, s.shape, 1)
        s = jnp.where(key_at <= query_at, s, -1e30)
        top = jnp.max(s, axis=1, keepdims=True)
        p = jnp.exp2(s - top).astype(BF16)
        acc = jnp.dot(p, here[:, HEAD_DIM:], preferred_element_type=F32)

        def step(kb, carry):
            top, acc = carry
            there = kvo[block(kb, TOK), :]
            s = lax.dot_general(q[...], there[:, :HEAD_DIM], along, preferred_element_type=F32)
            new = jnp.maximum(top, jnp.max(s, axis=1, keepdims=True))
            p = jnp.exp2(s - new).astype(BF16)
            acc = acc * jnp.exp2(top - new) + jnp.dot(p, there[:, HEAD_DIM:], preferred_element_type=F32)
            return new, acc

        top, acc = lax.fori_loop(0, row, step, (top, acc))
        mixed = (acc[:, :HEAD_DIM] / acc[:, HEAD_DIM:]).astype(BF16)
        a2[rows, block(g)] = jnp.concatenate([mixed[:B], mixed[B:]], axis=1)
        gather_send(1, a2, t)

    weight_pass(1, wout)
    weight_wait(1, wout)
    for t in range(CHUNKS):
        gather_pass(1, a2, t)
    for t in range(CHUNKS):
        gather_wait(1, a2, t)
        partial_send(1, a2, wout, stage2, got2, own2, t)
    for t in range(CHUNKS):
        out[pl.ds(t * B, B), :] = partial_sum(1, got2, own2, t).astype(BF16)

    for copy in sent:
        copy.wait_send()
    for t in range(CHUNKS):

        @pl.when(x != t)
        def _():
            kv_copy(t).wait_send()

    @pl.when(yh == 0)
    def _():
        kv_down().wait_send()

    @pl.when(yh == 1)
    def _():
        for copy in kv_relay():
            copy.wait_send()
        kv_across(1, above).wait_send()

    @pl.when(co == 0)
    def _():
        kv_across(0, row).wait_send()


def local_step(activations, norm_gain, w_query, w_key, w_value, w_out):
    cos, sin = rope_constants()
    dma = pltpu.SemaphoreType.DMA
    vmem = pl.BlockSpec(memory_space=pltpu.VMEM)
    hbm = pl.BlockSpec(memory_space=pl.ANY)
    return pl.pallas_call(
        kernel,
        out_shape=jax.ShapeDtypeStruct((TOK, B), BF16),
        in_specs=[vmem, vmem] + [hbm] * 6,
        out_specs=vmem,
        scratch_shapes=[
            pltpu.VMEM((TOK, 8 * B), BF16),
            pltpu.VMEM((TOK, 8 * B), BF16),
            pltpu.VMEM((8, B, 4 * B), BF16),
            pltpu.VMEM((8, B, B), BF16),
            pltpu.VMEM((8, B, 4 * B), BF16),
            pltpu.VMEM((3, TOK, B), BF16),
            pltpu.VMEM((3, TOK, B), BF16),
            pltpu.VMEM((4, TOK, B), BF16),
            pltpu.VMEM((4, TOK, B), BF16),
            pltpu.VMEM((TOK, B), F32),
            pltpu.VMEM((TOK, B), F32),
            pltpu.VMEM((TOK, B), BF16),
            pltpu.VMEM((4, B, B), BF16),
            pltpu.VMEM((B, B), F32),
            pltpu.VMEM((LENGTH, 3 * HEAD_DIM), BF16),
            pltpu.VMEM((TOK, 128), F32),
            pltpu.VMEM((TOK, HEAD_DIM), F32),
            pltpu.VMEM((TOK, HEAD_DIM), F32),
            pltpu.VMEM((2 * B, HEAD_DIM), BF16),
            pltpu.VMEM((8, 1, TOK), F32),
            pltpu.VMEM((4, 1, TOK), F32),
            dma((6,)),
            dma((2, CHUNKS, 8)),
            dma((2, CHUNKS, 8)),
            dma((8,)),
            dma((8,)),
            dma((4,)),
            dma((4,)),
            dma((2, 8)),
            dma((2, 2, 4)),
            dma((2, 2)),
            dma((2, 2)),
            dma((3,)),
            dma((3,)),
            dma((2, CHUNKS, 4)),
            dma((2, CHUNKS, 4)),
            dma((CHUNKS,)),
            dma((4,)),
            dma((8,)),
            dma((4, 4)),
            dma((2,)),
            dma((2,)),
        ],
        compiler_params=pltpu.CompilerParams(
            collective_id=0, has_side_effects=True, vmem_limit_bytes=58 * 2**20
        ),
    )(
        activations,
        norm_gain.reshape(1, B),
        w_query.reshape(2, 4, B, B),
        w_key.reshape(2, 4, B, 1024),
        w_value.reshape(2, 4, B, 1024),
        w_out.reshape(2, 4, B, B),
        cos,
        sin,
    )


def solution(mesh):
    placed = (
        P("row", "col"),
        P("col"),
        P("row", "col"),
        P("row", None),
        P("row", None),
        P("row", "col"),
    )
    return jax.shard_map(
        local_step, mesh=mesh, in_specs=placed, out_specs=P("row", "col"), check_vma=False
    )
```

```python
import functools

import jax
import jax.numpy as jnp
import numpy as np
from jax import lax
from jax.experimental import pallas as pl
from jax.experimental.pallas import tpu as pltpu
from jax.sharding import PartitionSpec as P

MESH = pl.DeviceIdType.MESH
HEAD_DIM = 128
TOK = 1024
B = 256
CHUNKS = TOK // B
LENGTH = 4096
D = 8192
SCALE = HEAD_DIM**-0.5 * 1.4426950408889634
F32 = jnp.float32
BF16 = jnp.bfloat16


def rope_constants():
    half = HEAD_DIM // 2
    frequency = np.exp(-np.log(500000.0) * (np.arange(half) * (2.0 / HEAD_DIM)))
    angles = np.arange(LENGTH)[:, None] * frequency[None, :]
    cos, sin = np.cos(angles), np.sin(angles)
    return (
        np.concatenate([cos, cos], 1).astype(np.float32),
        np.concatenate([-sin, sin], 1).astype(np.float32),
    )


def remote(src, dst, send, recv, device):
    return pltpu.make_async_remote_copy(
        src_ref=src, dst_ref=dst, send_sem=send, recv_sem=recv, device_id=device, device_id_type=MESH
    )


def block(i, size=B):
    return pl.ds(pl.multiple_of(i * size, size), size)


def kernel(
    act, gain, wq, wk, wv, wo, cos_all, sin_all, out,
    a1, a2, w, wkv, wout, stage1, stage2, got1, got2, own1, own2, kv_stage, kv_got, kv_own, kvo, inv, cos, sin, q,
    ss1, ss2,
    loc_sem, agy_s, agy_r, agz_s, agz_r, ss_s, ss_r, ssx_s, ssx_r, w_s, w_r, wf_s, wf_r, kvw_s, kvw_r, rs_s, rs_r, kvp_s, kvp_r, kvg_s,
    kvg_r, kvf_s, kvf_r,
):
    row, col = lax.axis_index("row"), lax.axis_index("col")
    yh, co = row // 2, row % 2
    z, yl, x = col // 8, (col // 4) % 2, col % 4
    g = z * 2 + yl

    def at(yh_, co_, z_, yl_, x_):
        return (yh_ * 2 + co_, z_ * 8 + yl_ * 4 + x_)

    z_peers = [at(yh, co, (z + d) % 4, yl, x) for d in (1, 3, 2)]
    yl_peer = at(yh, co, z, 1 - yl, x)
    x_at = [(x + d) % 4 for d in (1, 3, 2)]
    x_peers = [at(yh, co, z, yl, v) for v in x_at]
    y_peer = at(1 - yh, co, z, yl, x)
    sibling = at(yh, 1 - co, z, yl, x)

    barrier = pltpu.get_barrier_semaphore()
    everyone = z_peers + [yl_peer] + x_peers + [y_peer, sibling]
    for peer in everyone:
        pl.semaphore_signal(barrier, inc=1, device_id=peer, device_id_type=MESH)

    sent = []

    def send(src, dst, s, r, device):
        copy = remote(src, dst, s, r, device)
        copy.start()
        sent.append(copy)

    def arrived(dst, s, r):
        remote(dst, dst, s, r, sibling).wait_recv()

    local = [
        pltpu.make_async_copy(cos_all.at[block(row, TOK)], cos, loc_sem.at[0]),
        pltpu.make_async_copy(sin_all.at[block(row, TOK)], sin, loc_sem.at[1]),
        pltpu.make_async_copy(wk.at[:, x, :, block(g, 128)], wkv.at[pl.ds(2 * row, 2), :, pl.ds(0, 128)], loc_sem.at[2]),
        pltpu.make_async_copy(wv.at[:, x, :, block(g, 128)], wkv.at[pl.ds(2 * row, 2), :, pl.ds(128, 128)], loc_sem.at[3]),
        pltpu.make_async_copy(wq.at[:, x], w.at[pl.ds(2 * row, 2), :, block(x)], loc_sem.at[4]),
        pltpu.make_async_copy(wo.at[:, x], wout.at[pl.ds(2 * row, 2), :, block(x)], loc_sem.at[5]),
    ]
    for copy in local:
        copy.start()
    a1[:, block(g)] = (act[...].astype(F32) * gain[...].astype(F32)).astype(BF16)
    along = (((1,), (1,)), ((), ()))

    pl.semaphore_wait(barrier, len(everyone))

    other = z * 2 + 1 - yl

    def tile(a, t, who):
        return a.at[pl.ds(t * B, B), block(who)]

    def half(a, t, who, h):
        return a.at[pl.ds(t * B + h * (B // 2), B // 2), block(who)]

    def gather_first(phase, a, t):
        send(tile(a, t, g), tile(a, t, g), agy_s.at[phase, t], agy_r.at[phase, t], yl_peer)

    def gather_spread(phase, a, t, who, slot):
        for d, h in ((0, 0), (1, 1), (0, 1), (1, 0)):
            piece = half(a, t, who, h)
            send(piece, piece, agz_s.at[phase, t, slot, d * 2 + h], agz_r.at[phase, t, who, d * 2 + h], z_peers[d])

    def gather_second(phase, a, t):
        arrived(tile(a, t, other), agy_s.at[phase, t], agy_r.at[phase, t])
        gather_spread(phase, a, t, other, 1)

    def gather_relay(phase, a, t, same):
        y = yl if same else 1 - yl
        for d, h, to in ((3, 0, 0), (1, 1, 1)):
            who = ((z + d) % 4) * 2 + y
            piece = half(a, t, who, h)
            arrived(piece, agz_s.at[phase, t, 0, 0], agz_r.at[phase, t, who, to * 3])
            send(piece, piece, agz_s.at[phase, t, 2, to * 2 + int(same)], agz_r.at[phase, t, who, to * 3], z_peers[to])

    def gather_wait(phase, a, t):
        for y in range(2):
            for d, h, k in ((3, 1, 1), (1, 0, 2), (2, 0, 0), (2, 1, 3)):
                who = ((z + d) % 4) * 2 + y
                arrived(half(a, t, who, h), agz_s.at[phase, t, 0, 0], agz_r.at[phase, t, who, k])

    far_row = (1 - yh) * 2 + co

    def weight_piece(dst, r, xs):
        return dst.at[pl.ds(2 * r, 2), :, block(xs)]

    def weight_first(phase, src, dst):
        send(src.at[:, x], weight_piece(dst, row, x), w_s.at[phase, 3], w_r.at[phase, 1, x], y_peer)
        for k, (xd, peer) in enumerate(zip(x_at, x_peers)):
            send(src.at[:, xd], weight_piece(dst, row, x), w_s.at[phase, k], w_r.at[phase, 0, x], peer)

    def weight_relay(phase, dst, k):
        piece = weight_piece(dst, row, x_at[k])
        arrived(piece, w_s.at[phase, 0], w_r.at[phase, 0, x_at[k]])
        send(piece, piece, w_s.at[phase, 4 + k], w_r.at[phase, 1, x_at[k]], y_peer)

    def weight_near(phase, dst):
        local[4 + phase].wait()
        slab = dst.at[pl.ds(2 * row, 2)]
        send(slab, slab, wf_s.at[phase, 0], wf_r.at[phase, 0], sibling)

    def weight_far(phase, dst):
        for k, xs in enumerate([x] + x_at):
            piece = weight_piece(dst, far_row, xs)
            arrived(piece, w_s.at[phase, 0], w_r.at[phase, 1, xs])
            send(piece, piece, wf_s.at[phase, 1 + k], wf_r.at[phase, 1 + k], sibling)

    def weight_wait(phase, dst):
        arrived(dst.at[pl.ds(2 * (row + 1 - 2 * co), 2)], wf_s.at[phase, 0], wf_r.at[phase, 0])
        for k, xs in enumerate([x] + x_at):
            piece = weight_piece(dst, far_row + 1 - 2 * co, xs)
            arrived(piece, wf_s.at[phase, 1 + k], wf_r.at[phase, 1 + k])

    def kv_slab(r):
        return wkv.at[pl.ds(2 * r, 2)]

    def kv_weight_first():
        local[2].wait()
        local[3].wait()
        send(kv_slab(row), kv_slab(row), kvw_s.at[0], kvw_r.at[0], y_peer)
        send(kv_slab(row), kv_slab(row), kvw_s.at[1], kvw_r.at[1], sibling)

    def kv_weight_relay():
        arrived(kv_slab(far_row), kvw_s.at[0], kvw_r.at[0])
        send(kv_slab(far_row), kv_slab(far_row), kvw_s.at[2], kvw_r.at[2], sibling)

    def kv_weight_wait():
        arrived(kv_slab(row + 1 - 2 * co), kvw_s.at[1], kvw_r.at[1])
        arrived(kv_slab(far_row + 1 - 2 * co), kvw_s.at[2], kvw_r.at[2])

    def partial_send(phase, a, weights, stage, got, own, t):
        rows = pl.ds(t * B, B)
        for k, (xd, peer) in enumerate(zip(x_at, x_peers)):
            part = jnp.dot(
                a[rows, :], weights[:, :, block(xd)].reshape(8 * B, B), preferred_element_type=F32
            )
            stage[k, rows, :] = part.astype(BF16)
            send(stage.at[k, rows], got.at[x, rows], rs_s.at[phase, t, k], rs_r.at[phase, t, x], peer)
        own[rows, :] = jnp.dot(a[rows, :], weights[:, :, block(x)].reshape(8 * B, B), preferred_element_type=F32)

    def partial_sum(phase, got, own, t):
        rows = pl.ds(t * B, B)
        total = own[rows, :]
        for xs in x_at:
            arrived(got.at[xs, rows], rs_s.at[phase, t, 0], rs_r.at[phase, t, xs])
            total = total + got[xs, rows, :].astype(F32)
        return total

    def squares_first():
        wide = act[...].astype(F32)
        square = wide * wide
        high = square.astype(BF16)
        low = (square - high.astype(F32)).astype(BF16)
        ones = jnp.ones((8, B), BF16)
        sums = lax.dot_general(ones, high, along, preferred_element_type=F32) + lax.dot_general(
            ones, low, along, preferred_element_type=F32
        )
        ss1[g] = sums[0:1]
        for k, peer in enumerate([yl_peer] + z_peers):
            send(ss1.at[g], ss1.at[g], ss_s.at[k], ss_r.at[g], peer)

    def squares_relay():
        arrived(ss1.at[other], ss_s.at[0], ss_r.at[other])
        for k, peer in enumerate(z_peers):
            send(ss1.at[other], ss1.at[other], ss_s.at[4 + k], ss_r.at[other], peer)

    def squares_second():
        for d in (1, 3, 2):
            for y in range(2):
                who = ((z + d) % 4) * 2 + y
                arrived(ss1.at[who], ss_s.at[0], ss_r.at[who])
        ss2[x] = jnp.sum(ss1[...], axis=0)
        for k, peer in enumerate(x_peers):
            send(ss2.at[x], ss2.at[x], ssx_s.at[k], ssx_r.at[x], peer)

    def squares_wait():
        for xs in x_at:
            arrived(ss2.at[xs], ssx_s.at[0], ssx_r.at[xs])
        factor = lax.rsqrt(jnp.sum(ss2[...], axis=0) / D + 1e-05)
        for b in range(TOK // 128):
            inv[pl.ds(b * 128, 128), :] = jnp.broadcast_to(factor[:, b * 128 : (b + 1) * 128], (128, 128)).T

    def kv_copy(t):
        rows = pl.ds(t * B, B)
        return remote(kv_stage.at[rows], kv_got.at[x], kvp_s.at[t], kvp_r.at[x], at(yh, co, z, yl, t))

    def kv_part(t):
        rows = pl.ds(t * B, B)
        part = jnp.dot(a1[rows, :], wkv[...].reshape(8 * B, B), preferred_element_type=F32)
        kv_stage[rows, :] = part.astype(BF16)

        @pl.when(x != t)
        def _():
            kv_copy(t).start()

        @pl.when(x == t)
        def _():
            kv_own[...] = part

    gather_first(0, a1, 0)
    gather_spread(0, a1, 0, g, 0)
    weight_first(0, wq, w)
    gather_first(0, a1, 1)
    gather_spread(0, a1, 1, g, 0)
    kv_weight_first()
    for t in (2, 3):
        gather_first(0, a1, t)
        gather_spread(0, a1, t, g, 0)
    squares_first()
    kvo[:, 2 * HEAD_DIM :] = jnp.ones((LENGTH, HEAD_DIM), BF16)

    for t in range(CHUNKS):
        gather_second(0, a1, t)
        gather_relay(0, a1, t, True)
        if t == 0:
            weight_relay(0, w, 0)
            weight_relay(0, w, 1)
            squares_relay()
        if t == 1:
            weight_relay(0, w, 2)
            weight_near(0, w)
            kv_weight_relay()
            weight_first(1, wo, wout)
            squares_second()
        if t >= 1:
            gather_relay(0, a1, t - 1, False)
        if t == 2:
            kv_weight_wait()
        if t >= 2:
            gather_wait(0, a1, t - 2)
            kv_part(t - 2)
    gather_relay(0, a1, 3, False)
    gather_wait(0, a1, 2)
    kv_part(2)
    weight_far(0, w)
    weight_wait(0, w)
    partial_send(0, a1, w, stage1, got1, own1, 0)
    gather_wait(0, a1, 3)
    kv_part(3)
    partial_send(0, a1, w, stage1, got1, own1, 1)
    for k in range(3):
        weight_relay(1, wout, k)
    weight_near(1, wout)
    squares_wait()
    partial_send(0, a1, w, stage1, got1, own1, 2)
    local[0].wait()
    local[1].wait()

    mine = block(x)
    total = kv_own[...]
    for xs in x_at:
        arrived(kv_got.at[xs], kvp_s.at[0], kvp_r.at[xs])
        total = total + kv_got[xs].astype(F32)
    scale = inv[mine, :]
    key = total[:, :HEAD_DIM] * scale
    key = (key * cos[mine, :] + pltpu.roll(key, HEAD_DIM // 2, 1) * sin[mine, :]).astype(BF16)
    value = (total[:, HEAD_DIM:] * scale).astype(BF16)
    kvo[block(row * 4 + x), 0 : 2 * HEAD_DIM] = jnp.concatenate([key, value], axis=1)

    def quarter(r, xs):
        return kvo.at[block(r * 4 + xs), pl.ds(0, 2 * HEAD_DIM)]

    def whole(r):
        return kvo.at[block(r, TOK), pl.ds(0, 2 * HEAD_DIM)]

    def kv_down():
        return remote(quarter(row, x), quarter(row, x), kvg_s.at[3], kvg_r.at[row, x], y_peer)

    def kv_across(which, r):
        return remote(whole(r), whole(r), kvf_s.at[which], kvf_r.at[which], sibling)

    @pl.when(yh == 0)
    def _():
        kv_down().start()

    for k, peer in enumerate(x_peers):
        send(quarter(row, x), quarter(row, x), kvg_s.at[k], kvg_r.at[row, x], peer)

    above = row - 2

    def kv_relay():
        return [
            remote(quarter(above, x), quarter(above, x), kvg_s.at[4 + k], kvg_r.at[above, x], peer)
            for k, peer in enumerate(x_peers)
        ]

    @pl.when(yh == 1)
    def _():
        arrived(quarter(above, x), kvg_s.at[0], kvg_r.at[above, x])
        for copy in kv_relay():
            copy.start()

    partial_send(0, a1, w, stage1, got1, own1, 3)
    for xs in x_at:
        arrived(quarter(row, xs), kvg_s.at[0], kvg_r.at[row, xs])

    @pl.when(co == 0)
    def _():
        kv_across(0, row).start()

    @pl.when(yh == 1)
    def _():
        for xs in x_at:
            arrived(quarter(above, xs), kvg_s.at[0], kvg_r.at[above, xs])
        kv_across(1, above).start()
        arrived(whole(above + 1 - 2 * co), kvf_s.at[1], kvf_r.at[1])

    @pl.when(co == 1)
    def _():
        arrived(whole(row - 1), kvf_s.at[0], kvf_r.at[0])

    for t in range(CHUNKS):
        rows = pl.ds(t * B, B)
        total = partial_sum(0, got1, own1, t)
        scale = inv[rows, :] * SCALE
        for h in range(2):
            part = total[:, h * HEAD_DIM : (h + 1) * HEAD_DIM] * scale
            part = part * cos[rows, :] + pltpu.roll(part, HEAD_DIM // 2, 1) * sin[rows, :]
            q[pl.ds(h * B, B), :] = part.astype(BF16)
        width = (t + 1) * B
        here = kvo[pl.ds(pl.multiple_of(row * TOK, TOK), width), :]
        queries = q[...]
        s = lax.dot_general(queries, here[:, :HEAD_DIM], along, preferred_element_type=F32)
        query_at = lax.broadcasted_iota(jnp.int32, s.shape, 0) % B + t * B
        key_at = lax.broadcasted_iota(jnp.int32, s.shape, 1)
        s = jnp.where(key_at <= query_at, s, -1e30)
        top = jnp.max(s, axis=1, keepdims=True)
        p = jnp.exp2(s - top).astype(BF16)
        acc = jnp.dot(p, here[:, HEAD_DIM:], preferred_element_type=F32)

        def step(kb, carry):
            top, acc = carry
            there = kvo[block(kb, TOK), :]
            s = lax.dot_general(q[...], there[:, :HEAD_DIM], along, preferred_element_type=F32)
            new = jnp.maximum(top, jnp.max(s, axis=1, keepdims=True))
            p = jnp.exp2(s - new).astype(BF16)
            acc = acc * jnp.exp2(top - new) + jnp.dot(p, there[:, HEAD_DIM:], preferred_element_type=F32)
            return new, acc

        top, acc = lax.fori_loop(0, row, step, (top, acc))
        mixed = (acc[:, :HEAD_DIM] / acc[:, HEAD_DIM:]).astype(BF16)
        a2[rows, block(g)] = jnp.concatenate([mixed[:B], mixed[B:]], axis=1)
        gather_first(1, a2, t)
        gather_spread(1, a2, t, g, 0)
        if t >= 1:
            gather_second(1, a2, t - 1)
            gather_relay(1, a2, t - 1, True)
        if t >= 2:
            gather_relay(1, a2, t - 2, False)

    gather_second(1, a2, 3)
    gather_relay(1, a2, 3, True)
    gather_relay(1, a2, 2, False)
    weight_far(1, wout)
    weight_wait(1, wout)
    gather_wait(1, a2, 0)
    partial_send(1, a2, wout, stage2, got2, own2, 0)
    gather_relay(1, a2, 3, False)
    for t in range(CHUNKS):
        if t >= 1:
            gather_wait(1, a2, t)
            partial_send(1, a2, wout, stage2, got2, own2, t)
    for t in range(CHUNKS):
        out[pl.ds(t * B, B), :] = partial_sum(1, got2, own2, t).astype(BF16)

    for copy in sent:
        copy.wait_send()
    for t in range(CHUNKS):

        @pl.when(x != t)
        def _():
            kv_copy(t).wait_send()

    @pl.when(yh == 0)
    def _():
        kv_down().wait_send()

    @pl.when(yh == 1)
    def _():
        for copy in kv_relay():
            copy.wait_send()
        kv_across(1, above).wait_send()

    @pl.when(co == 0)
    def _():
        kv_across(0, row).wait_send()


def local_step(activations, norm_gain, w_query, w_key, w_value, w_out):
    cos, sin = rope_constants()
    dma = pltpu.SemaphoreType.DMA
    vmem = pl.BlockSpec(memory_space=pltpu.VMEM)
    hbm = pl.BlockSpec(memory_space=pl.ANY)
    return pl.pallas_call(
        kernel,
        out_shape=jax.ShapeDtypeStruct((TOK, B), BF16),
        in_specs=[vmem, vmem] + [hbm] * 6,
        out_specs=vmem,
        scratch_shapes=[
            pltpu.VMEM((TOK, 8 * B), BF16),
            pltpu.VMEM((TOK, 8 * B), BF16),
            pltpu.VMEM((8, B, 4 * B), BF16),
            pltpu.VMEM((8, B, B), BF16),
            pltpu.VMEM((8, B, 4 * B), BF16),
            pltpu.VMEM((3, TOK, B), BF16),
            pltpu.VMEM((3, TOK, B), BF16),
            pltpu.VMEM((4, TOK, B), BF16),
            pltpu.VMEM((4, TOK, B), BF16),
            pltpu.VMEM((TOK, B), F32),
            pltpu.VMEM((TOK, B), F32),
            pltpu.VMEM((TOK, B), BF16),
            pltpu.VMEM((4, B, B), BF16),
            pltpu.VMEM((B, B), F32),
            pltpu.VMEM((LENGTH, 3 * HEAD_DIM), BF16),
            pltpu.VMEM((TOK, 128), F32),
            pltpu.VMEM((TOK, HEAD_DIM), F32),
            pltpu.VMEM((TOK, HEAD_DIM), F32),
            pltpu.VMEM((2 * B, HEAD_DIM), BF16),
            pltpu.VMEM((8, 1, TOK), F32),
            pltpu.VMEM((4, 1, TOK), F32),
            dma((6,)),
            dma((2, CHUNKS)),
            dma((2, CHUNKS)),
            dma((2, CHUNKS, 3, 4)),
            dma((2, CHUNKS, 8, 4)),
            dma((8,)),
            dma((8,)),
            dma((4,)),
            dma((4,)),
            dma((2, 8)),
            dma((2, 2, 4)),
            dma((2, 5)),
            dma((2, 5)),
            dma((3,)),
            dma((3,)),
            dma((2, CHUNKS, 4)),
            dma((2, CHUNKS, 4)),
            dma((CHUNKS,)),
            dma((4,)),
            dma((8,)),
            dma((4, 4)),
            dma((2,)),
            dma((2,)),
        ],
        compiler_params=pltpu.CompilerParams(
            collective_id=0, has_side_effects=True, vmem_limit_bytes=58 * 2**20
        ),
    )(
        activations,
        norm_gain.reshape(1, B),
        w_query.reshape(2, 4, B, B),
        w_key.reshape(2, 4, B, 1024),
        w_value.reshape(2, 4, B, 1024),
        w_out.reshape(2, 4, B, B),
        cos,
        sin,
    )


def solution(mesh):
    placed = (
        P("row", "col"),
        P("col"),
        P("row", "col"),
        P("row", None),
        P("row", None),
        P("row", "col"),
    )
    return jax.shard_map(
        local_step, mesh=mesh, in_specs=placed, out_specs=P("row", "col"), check_vma=False
    )
```

```python
import functools

import jax
import jax.numpy as jnp
import numpy as np
from jax import lax
from jax.experimental import pallas as pl
from jax.experimental.pallas import tpu as pltpu
from jax.sharding import PartitionSpec as P

MESH = pl.DeviceIdType.MESH
HEAD_DIM = 128
TOK = 1024
B = 256
CHUNKS = TOK // B
SUB = B // 4
LENGTH = 4096
D = 8192
SCALE = HEAD_DIM**-0.5 * 1.4426950408889634
F32 = jnp.float32
BF16 = jnp.bfloat16


def rope_constants():
    half = HEAD_DIM // 2
    frequency = np.exp(-np.log(500000.0) * (np.arange(half) * (2.0 / HEAD_DIM)))
    angles = np.arange(LENGTH)[:, None] * frequency[None, :]
    cos, sin = np.cos(angles), np.sin(angles)
    return (
        np.concatenate([cos, cos], 1).astype(np.float32),
        np.concatenate([-sin, sin], 1).astype(np.float32),
    )


def remote(src, dst, send, recv, device):
    return pltpu.make_async_remote_copy(
        src_ref=src, dst_ref=dst, send_sem=send, recv_sem=recv, device_id=device, device_id_type=MESH
    )


def block(i, size=B):
    return pl.ds(pl.multiple_of(i * size, size), size)


def kernel(
    act, gain, wq, wk, wv, wo, cos_all, sin_all, out,
    a1, a2, w, wkv, wout, stage1, stage2, got1, got2, own1, own2, kv_stage, kv_got, kv_own, kvo, inv, cos, sin, q,
    ss1, ss2,
    loc_sem, agy_s, agy_r, agz_s, agz_r, ss_s, ss_r, ssx_s, ssx_r, w_s, w_r, wf_s, wf_r, kvw_s, kvw_r, rs_s, rs_r, kvp_s, kvp_r, kvg_s,
    kvg_r, kvf_s, kvf_r,
):
    row, col = lax.axis_index("row"), lax.axis_index("col")
    yh, co = row // 2, row % 2
    z, yl, x = col // 8, (col // 4) % 2, col % 4
    g = z * 2 + yl

    def at(yh_, co_, z_, yl_, x_):
        return (yh_ * 2 + co_, z_ * 8 + yl_ * 4 + x_)

    z_peers = [at(yh, co, (z + d) % 4, yl, x) for d in (1, 3, 2)]
    yl_peer = at(yh, co, z, 1 - yl, x)
    x_at = [(x + d) % 4 for d in (1, 3, 2)]
    x_peers = [at(yh, co, z, yl, v) for v in x_at]
    y_peer = at(1 - yh, co, z, yl, x)
    sibling = at(yh, 1 - co, z, yl, x)

    barrier = pltpu.get_barrier_semaphore()
    everyone = z_peers + [yl_peer] + x_peers + [y_peer, sibling]
    for peer in everyone:
        pl.semaphore_signal(barrier, inc=1, device_id=peer, device_id_type=MESH)

    sent = []

    def send(src, dst, s, r, device):
        copy = remote(src, dst, s, r, device)
        copy.start()
        sent.append(copy)

    def arrived(dst, s, r):
        remote(dst, dst, s, r, sibling).wait_recv()

    local = [
        pltpu.make_async_copy(cos_all.at[block(row, TOK)], cos, loc_sem.at[0]),
        pltpu.make_async_copy(sin_all.at[block(row, TOK)], sin, loc_sem.at[1]),
        pltpu.make_async_copy(wk.at[:, x, :, block(g, 128)], wkv.at[pl.ds(2 * row, 2), :, pl.ds(0, 128)], loc_sem.at[2]),
        pltpu.make_async_copy(wv.at[:, x, :, block(g, 128)], wkv.at[pl.ds(2 * row, 2), :, pl.ds(128, 128)], loc_sem.at[3]),
        pltpu.make_async_copy(wq.at[:, x], w.at[pl.ds(2 * row, 2), :, block(x)], loc_sem.at[4]),
        pltpu.make_async_copy(wo.at[:, x], wout.at[pl.ds(2 * row, 2), :, block(x)], loc_sem.at[5]),
    ]
    for copy in local:
        copy.start()
    a1[:, block(g)] = (act[...].astype(F32) * gain[...].astype(F32)).astype(BF16)
    along = (((1,), (1,)), ((), ()))

    wide = act[...].astype(F32)
    square = wide * wide
    high = square.astype(BF16)
    low = (square - high.astype(F32)).astype(BF16)
    ones = jnp.ones((8, B), BF16)
    sums = lax.dot_general(ones, high, along, preferred_element_type=F32) + lax.dot_general(
        ones, low, along, preferred_element_type=F32
    )
    ss1[g] = sums[0:1]
    kvo[:, 2 * HEAD_DIM :] = jnp.ones((LENGTH, HEAD_DIM), BF16)

    pl.semaphore_wait(barrier, len(everyone))

    other = z * 2 + 1 - yl

    def tile(a, t, who):
        return a.at[pl.ds(t * B, B), block(who)]

    def half(a, t, who, h):
        return a.at[pl.ds(t * B + h * (B // 2), B // 2), block(who)]

    def gather_first(phase, a, t):
        send(tile(a, t, g), tile(a, t, g), agy_s.at[phase, t], agy_r.at[phase, t], yl_peer)

    def gather_spread(phase, a, t, who, slot):
        for d, h in ((0, 0), (1, 1), (0, 1), (1, 0)):
            piece = half(a, t, who, h)
            send(piece, piece, agz_s.at[phase, t, slot, d * 2 + h], agz_r.at[phase, t, who, d * 2 + h], z_peers[d])

    def gather_second(phase, a, t):
        arrived(tile(a, t, other), agy_s.at[phase, t], agy_r.at[phase, t])
        gather_spread(phase, a, t, other, 1)

    def gather_relay(phase, a, t, same):
        y = yl if same else 1 - yl
        for d, h, to in ((3, 0, 0), (1, 1, 1)):
            who = ((z + d) % 4) * 2 + y
            piece = half(a, t, who, h)
            arrived(piece, agz_s.at[phase, t, 0, 0], agz_r.at[phase, t, who, to * 3])
            send(piece, piece, agz_s.at[phase, t, 2, to * 2 + int(same)], agz_r.at[phase, t, who, to * 3], z_peers[to])

    def gather_wait(phase, a, t):
        for y in range(2):
            for d, h, k in ((3, 1, 1), (1, 0, 2), (2, 0, 0), (2, 1, 3)):
                who = ((z + d) % 4) * 2 + y
                arrived(half(a, t, who, h), agz_s.at[phase, t, 0, 0], agz_r.at[phase, t, who, k])

    far_row = (1 - yh) * 2 + co

    def weight_piece(dst, r, xs):
        return dst.at[pl.ds(2 * r, 2), :, block(xs)]

    def weight_first(phase, src, dst):
        for k, (xd, peer) in enumerate(zip(x_at, x_peers)):
            send(src.at[:, xd], weight_piece(dst, row, x), w_s.at[phase, k], w_r.at[phase, 0, x], peer)

    def weight_down(phase, src, dst):
        send(src.at[:, x], weight_piece(dst, row, x), w_s.at[phase, 3], w_r.at[phase, 1, x], y_peer)

    def weight_relay(phase, dst, k):
        piece = weight_piece(dst, row, x_at[k])
        arrived(piece, w_s.at[phase, 0], w_r.at[phase, 0, x_at[k]])
        send(piece, piece, w_s.at[phase, 4 + k], w_r.at[phase, 1, x_at[k]], y_peer)

    def weight_near(phase, dst):
        local[4 + phase].wait()
        slab = dst.at[pl.ds(2 * row, 2)]
        send(slab, slab, wf_s.at[phase, 0], wf_r.at[phase, 0], sibling)

    def weight_far(phase, dst):
        for k, xs in enumerate([x] + x_at):
            piece = weight_piece(dst, far_row, xs)
            arrived(piece, w_s.at[phase, 0], w_r.at[phase, 1, xs])
            send(piece, piece, wf_s.at[phase, 1 + k], wf_r.at[phase, 1 + k], sibling)

    def weight_wait(phase, dst):
        arrived(dst.at[pl.ds(2 * (row + 1 - 2 * co), 2)], wf_s.at[phase, 0], wf_r.at[phase, 0])
        for k, xs in enumerate([x] + x_at):
            piece = weight_piece(dst, far_row + 1 - 2 * co, xs)
            arrived(piece, wf_s.at[phase, 1 + k], wf_r.at[phase, 1 + k])

    def kv_slab(r):
        return wkv.at[pl.ds(2 * r, 2)]

    def kv_weight_first():
        local[2].wait()
        local[3].wait()
        send(kv_slab(row), kv_slab(row), kvw_s.at[0], kvw_r.at[0], y_peer)
        send(kv_slab(row), kv_slab(row), kvw_s.at[1], kvw_r.at[1], sibling)

    def kv_weight_relay():
        arrived(kv_slab(far_row), kvw_s.at[0], kvw_r.at[0])
        send(kv_slab(far_row), kv_slab(far_row), kvw_s.at[2], kvw_r.at[2], sibling)

    def kv_weight_wait():
        arrived(kv_slab(row + 1 - 2 * co), kvw_s.at[1], kvw_r.at[1])
        arrived(kv_slab(far_row + 1 - 2 * co), kvw_s.at[2], kvw_r.at[2])

    def partial_one(a, weights, t, xd):
        return jnp.dot(
            a[pl.ds(t * B, B), :], weights[:, :, block(xd)].reshape(8 * B, B), preferred_element_type=F32
        )

    def partial_copy(phase, stage, got, t, k):
        rows = pl.ds(t * B, B)
        send(stage.at[k, rows], got.at[x, rows], rs_s.at[phase, t, k], rs_r.at[phase, t, x], x_peers[k])

    def partial_make(phase, a, weights, stage, got, own, t):
        rows = pl.ds(t * B, B)
        for k, xd in enumerate(x_at):
            stage[k, rows, :] = partial_one(a, weights, t, xd).astype(BF16)
        own[rows, :] = partial_one(a, weights, t, x)

    def partial_start(phase, stage, got, t):
        for k in range(3):
            partial_copy(phase, stage, got, t, k)

    def partial_send(phase, a, weights, stage, got, own, t):
        partial_make(phase, a, weights, stage, got, own, t)
        partial_start(phase, stage, got, t)

    def partial_sum(phase, got, own, t):
        rows = pl.ds(t * B, B)
        total = own[rows, :]
        for xs in x_at:
            arrived(got.at[xs, rows], rs_s.at[phase, t, 0], rs_r.at[phase, t, xs])
            total = total + got[xs, rows, :].astype(F32)
        return total

    def squares_first():
        for k, peer in enumerate([yl_peer] + z_peers):
            send(ss1.at[g], ss1.at[g], ss_s.at[k], ss_r.at[g], peer)

    def squares_relay():
        arrived(ss1.at[other], ss_s.at[0], ss_r.at[other])
        for k, peer in enumerate(z_peers):
            send(ss1.at[other], ss1.at[other], ss_s.at[4 + k], ss_r.at[other], peer)

    def squares_second():
        for d in (1, 3, 2):
            for y in range(2):
                who = ((z + d) % 4) * 2 + y
                arrived(ss1.at[who], ss_s.at[0], ss_r.at[who])
        ss2[x] = jnp.sum(ss1[...], axis=0)
        for k, peer in enumerate(x_peers):
            send(ss2.at[x], ss2.at[x], ssx_s.at[k], ssx_r.at[x], peer)

    def squares_wait():
        for xs in x_at:
            arrived(ss2.at[xs], ssx_s.at[0], ssx_r.at[xs])
        factor = lax.rsqrt(jnp.sum(ss2[...], axis=0) / D + 1e-05)
        for b in range(TOK // 128):
            inv[pl.ds(b * 128, 128), :] = jnp.broadcast_to(factor[:, b * 128 : (b + 1) * 128], (128, 128)).T

    above = row - 2

    def kv_part(t):
        rows = pl.ds(t * B, B)
        part = jnp.dot(a1[rows, :], wkv[...].reshape(8 * B, B), preferred_element_type=F32)
        kv_stage[rows, :] = part.astype(BF16)
        kv_own[t] = part
        for k, xd in enumerate(x_at):
            piece = kv_stage.at[pl.ds(pl.multiple_of(t * B + xd * SUB, SUB), SUB)]
            send(piece, kv_got.at[t, x], kvp_s.at[t, k], kvp_r.at[t, x], x_peers[k])

    def kv_piece(r, t, xs):
        return kvo.at[pl.ds(pl.multiple_of(r * TOK + t * B + xs * SUB, SUB), SUB), pl.ds(0, 2 * HEAD_DIM)]

    def kv_down(t):
        return remote(kv_piece(row, t, x), kv_piece(row, t, x), kvg_s.at[t, 3], kvg_r.at[1, t, x], y_peer)

    def kv_reduce(t):
        total = kv_own[t, block(x, SUB), :]
        for k, xs in enumerate(x_at):
            arrived(kv_got.at[t, xs], kvp_s.at[t, k], kvp_r.at[t, xs])
            total = total + kv_got[t, xs].astype(F32)
        mine = pl.ds(pl.multiple_of(t * B + x * SUB, SUB), SUB)
        scale = inv[mine, :]
        key = total[:, :HEAD_DIM] * scale
        key = (key * cos[mine, :] + pltpu.roll(key, HEAD_DIM // 2, 1) * sin[mine, :]).astype(BF16)
        value = (total[:, HEAD_DIM:] * scale).astype(BF16)
        kvo[pl.ds(pl.multiple_of(row * TOK + t * B + x * SUB, SUB), SUB), 0 : 2 * HEAD_DIM] = jnp.concatenate(
            [key, value], axis=1
        )

        @pl.when(yh == 0)
        def _():
            kv_down(t).start()

        for k, peer in enumerate(x_peers):
            send(kv_piece(row, t, x), kv_piece(row, t, x), kvg_s.at[t, k], kvg_r.at[0, t, x], peer)

    def kv_relay_copies(t):
        piece = kv_piece(above, t, x)
        return [remote(piece, piece, kvg_s.at[t, 4 + k], kvg_r.at[1, t, x], peer) for k, peer in enumerate(x_peers)]

    def kv_relay(t):
        @pl.when(yh == 1)
        def _():
            arrived(kv_piece(above, t, x), kvg_s.at[t, 0], kvg_r.at[1, t, x])
            for copy in kv_relay_copies(t):
                copy.start()

    def kv_whole(r):
        return kvo.at[block(r, TOK), pl.ds(0, 2 * HEAD_DIM)]

    def kv_across(which, r):
        return remote(kv_whole(r), kv_whole(r), kvf_s.at[which], kvf_r.at[which], sibling)

    def kv_own_wait():
        for t in range(CHUNKS):
            for xs in x_at:
                arrived(kv_piece(row, t, xs), kvg_s.at[t, 0], kvg_r.at[0, t, xs])

        @pl.when(co == 0)
        def _():
            kv_across(0, row).start()

    def kv_rest_wait():
        @pl.when(yh == 1)
        def _():
            for t in range(CHUNKS):
                for xs in x_at:
                    arrived(kv_piece(above, t, xs), kvg_s.at[t, 0], kvg_r.at[1, t, xs])
            kv_across(1, above).start()
            arrived(kv_whole(above + 1 - 2 * co), kvf_s.at[1], kvf_r.at[1])

        @pl.when(co == 1)
        def _():
            arrived(kv_whole(row - 1), kvf_s.at[0], kvf_r.at[0])

    gather_first(0, a1, 0)
    squares_first()
    gather_spread(0, a1, 0, g, 0)
    gather_first(0, a1, 1)
    gather_spread(0, a1, 1, g, 0)
    weight_first(0, wq, w)
    kv_weight_first()
    gather_first(0, a1, 2)
    gather_first(0, a1, 3)
    weight_down(0, wq, w)
    weight_first(1, wo, wout)

    def gather_turn(phase, a, t):
        gather_second(phase, a, t)
        gather_relay(phase, a, t, True)
        gather_relay(phase, a, t, False)

    gather_second(0, a1, 0)
    squares_relay()
    gather_relay(0, a1, 0, True)
    gather_relay(0, a1, 0, False)
    gather_spread(0, a1, 2, g, 0)
    weight_relay(0, w, 0)
    weight_relay(0, w, 1)

    gather_turn(0, a1, 1)
    gather_spread(0, a1, 3, g, 0)
    kv_weight_relay()
    weight_relay(0, w, 2)
    weight_near(0, w)
    squares_second()

    gather_second(0, a1, 2)
    gather_relay(0, a1, 2, True)
    kv_weight_wait()
    gather_wait(0, a1, 0)
    kv_part(0)
    gather_relay(0, a1, 2, False)

    gather_second(0, a1, 3)
    gather_relay(0, a1, 3, True)
    gather_wait(0, a1, 1)
    kv_part(1)
    local[0].wait()
    local[1].wait()
    squares_wait()
    kv_reduce(0)
    gather_relay(0, a1, 3, False)

    gather_wait(0, a1, 2)
    kv_part(2)
    kv_reduce(1)
    gather_wait(0, a1, 3)
    kv_part(3)
    kv_reduce(2)
    kv_reduce(3)
    for t in range(3):
        kv_relay(t)

    weight_far(0, w)
    weight_wait(0, w)
    partial_make(0, a1, w, stage1, got1, own1, 0)
    kv_relay(3)
    partial_start(0, stage1, got1, 0)
    weight_down(1, wo, wout)
    weight_relay(1, wout, 0)
    for t in range(1, CHUNKS):
        partial_make(0, a1, w, stage1, got1, own1, t)
    kv_own_wait()

    for t in range(CHUNKS):
        rows = pl.ds(t * B, B)
        total = partial_sum(0, got1, own1, t)
        scale = inv[rows, :] * SCALE
        for h in range(2):
            part = total[:, h * HEAD_DIM : (h + 1) * HEAD_DIM] * scale
            part = part * cos[rows, :] + pltpu.roll(part, HEAD_DIM // 2, 1) * sin[rows, :]
            q[pl.ds(h * B, B), :] = part.astype(BF16)
        width = (t + 1) * B
        here = kvo[pl.ds(pl.multiple_of(row * TOK, TOK), width), :]
        queries = q[...]
        s = lax.dot_general(queries, here[:, :HEAD_DIM], along, preferred_element_type=F32)
        query_at = lax.broadcasted_iota(jnp.int32, s.shape, 0) % B + t * B
        key_at = lax.broadcasted_iota(jnp.int32, s.shape, 1)
        s = jnp.where(key_at <= query_at, s, -1e30)
        top = jnp.max(s, axis=1, keepdims=True)
        p = jnp.exp2(s - top).astype(BF16)
        acc = jnp.dot(p, here[:, HEAD_DIM:], preferred_element_type=F32)

        if t == 0:
            kv_rest_wait()
            for v in range(1, CHUNKS):
                partial_start(0, stage1, got1, v)

        def step(kb, carry):
            top, acc = carry
            there = kvo[block(kb, TOK), :]
            s = lax.dot_general(q[...], there[:, :HEAD_DIM], along, preferred_element_type=F32)
            new = jnp.maximum(top, jnp.max(s, axis=1, keepdims=True))
            p = jnp.exp2(s - new).astype(BF16)
            acc = acc * jnp.exp2(top - new) + jnp.dot(p, there[:, HEAD_DIM:], preferred_element_type=F32)
            return new, acc

        top, acc = lax.fori_loop(0, row, step, (top, acc))
        mixed = (acc[:, :HEAD_DIM] / acc[:, HEAD_DIM:]).astype(BF16)
        a2[rows, block(g)] = jnp.concatenate([mixed[:B], mixed[B:]], axis=1)
        gather_first(1, a2, t)
        gather_spread(1, a2, t, g, 0)
        if t == 0:
            weight_relay(1, wout, 1)
        if t == 1:
            weight_relay(1, wout, 2)
            weight_near(1, wout)
        if t == 2:
            gather_relay(1, a2, 0, False)
        if t >= 1:
            gather_second(1, a2, t - 1)
            gather_relay(1, a2, t - 1, True)

    gather_relay(1, a2, 1, False)
    weight_far(1, wout)
    weight_wait(1, wout)
    gather_wait(1, a2, 0)
    partial_send(1, a2, wout, stage2, got2, own2, 0)
    gather_second(1, a2, 3)
    gather_relay(1, a2, 2, False)
    gather_relay(1, a2, 3, True)
    gather_wait(1, a2, 1)
    partial_send(1, a2, wout, stage2, got2, own2, 1)
    gather_relay(1, a2, 3, False)
    gather_wait(1, a2, 2)
    partial_send(1, a2, wout, stage2, got2, own2, 2)
    out[pl.ds(0, B), :] = partial_sum(1, got2, own2, 0).astype(BF16)
    gather_wait(1, a2, 3)
    partial_send(1, a2, wout, stage2, got2, own2, 3)
    for t in range(1, CHUNKS):
        out[pl.ds(t * B, B), :] = partial_sum(1, got2, own2, t).astype(BF16)

    for copy in sent:
        copy.wait_send()

    @pl.when(yh == 0)
    def _():
        for t in range(CHUNKS):
            kv_down(t).wait_send()

    @pl.when(yh == 1)
    def _():
        for t in range(CHUNKS):
            for copy in kv_relay_copies(t):
                copy.wait_send()
        kv_across(1, above).wait_send()

    @pl.when(co == 0)
    def _():
        kv_across(0, row).wait_send()


def local_step(activations, norm_gain, w_query, w_key, w_value, w_out):
    cos, sin = rope_constants()
    dma = pltpu.SemaphoreType.DMA
    vmem = pl.BlockSpec(memory_space=pltpu.VMEM)
    hbm = pl.BlockSpec(memory_space=pl.ANY)
    return pl.pallas_call(
        kernel,
        out_shape=jax.ShapeDtypeStruct((TOK, B), BF16),
        in_specs=[vmem, vmem] + [hbm] * 6,
        out_specs=vmem,
        scratch_shapes=[
            pltpu.VMEM((TOK, 8 * B), BF16),
            pltpu.VMEM((TOK, 8 * B), BF16),
            pltpu.VMEM((8, B, 4 * B), BF16),
            pltpu.VMEM((8, B, B), BF16),
            pltpu.VMEM((8, B, 4 * B), BF16),
            pltpu.VMEM((3, TOK, B), BF16),
            pltpu.VMEM((3, TOK, B), BF16),
            pltpu.VMEM((4, TOK, B), BF16),
            pltpu.VMEM((4, TOK, B), BF16),
            pltpu.VMEM((TOK, B), F32),
            pltpu.VMEM((TOK, B), F32),
            pltpu.VMEM((TOK, B), BF16),
            pltpu.VMEM((CHUNKS, 4, SUB, B), BF16),
            pltpu.VMEM((CHUNKS, B, B), F32),
            pltpu.VMEM((LENGTH, 3 * HEAD_DIM), BF16),
            pltpu.VMEM((TOK, 128), F32),
            pltpu.VMEM((TOK, HEAD_DIM), F32),
            pltpu.VMEM((TOK, HEAD_DIM), F32),
            pltpu.VMEM((2 * B, HEAD_DIM), BF16),
            pltpu.VMEM((8, 1, TOK), F32),
            pltpu.VMEM((4, 1, TOK), F32),
            dma((6,)),
            dma((2, CHUNKS)),
            dma((2, CHUNKS)),
            dma((2, CHUNKS, 3, 4)),
            dma((2, CHUNKS, 8, 4)),
            dma((8,)),
            dma((8,)),
            dma((4,)),
            dma((4,)),
            dma((2, 8)),
            dma((2, 2, 4)),
            dma((2, 5)),
            dma((2, 5)),
            dma((3,)),
            dma((3,)),
            dma((2, CHUNKS, 4)),
            dma((2, CHUNKS, 4)),
            dma((CHUNKS, 4)),
            dma((CHUNKS, 4)),
            dma((CHUNKS, 8)),
            dma((2, CHUNKS, 4)),
            dma((2,)),
            dma((2,)),
        ],
        compiler_params=pltpu.CompilerParams(
            collective_id=0, has_side_effects=True, vmem_limit_bytes=58 * 2**20
        ),
    )(
        activations,
        norm_gain.reshape(1, B),
        w_query.reshape(2, 4, B, B),
        w_key.reshape(2, 4, B, 1024),
        w_value.reshape(2, 4, B, 1024),
        w_out.reshape(2, 4, B, B),
        cos,
        sin,
    )


def solution(mesh):
    placed = (
        P("row", "col"),
        P("col"),
        P("row", "col"),
        P("row", None),
        P("row", None),
        P("row", "col"),
    )
    return jax.shard_map(
        local_step, mesh=mesh, in_specs=placed, out_specs=P("row", "col"), check_vma=False
    )
```

```python
import functools

import jax
import jax.numpy as jnp
import numpy as np
from jax import lax
from jax.experimental import pallas as pl
from jax.experimental.pallas import tpu as pltpu
from jax.sharding import PartitionSpec as P

MESH = pl.DeviceIdType.MESH
HEAD_DIM = 128
TOK = 1024
B = 256
CHUNKS = TOK // B
HB = B // 2
TURNS = TOK // HB
SUB = B // 4
LENGTH = 4096
D = 8192
SCALE = HEAD_DIM**-0.5 * 1.4426950408889634
F32 = jnp.float32
BF16 = jnp.bfloat16


def rope_constants():
    half = HEAD_DIM // 2
    frequency = np.exp(-np.log(500000.0) * (np.arange(half) * (2.0 / HEAD_DIM)))
    angles = np.arange(LENGTH)[:, None] * frequency[None, :]
    cos, sin = np.cos(angles), np.sin(angles)
    return (
        np.concatenate([cos, cos], 1).astype(np.float32),
        np.concatenate([-sin, sin], 1).astype(np.float32),
    )


def remote(src, dst, send, recv, device):
    return pltpu.make_async_remote_copy(
        src_ref=src, dst_ref=dst, send_sem=send, recv_sem=recv, device_id=device, device_id_type=MESH
    )


def block(i, size=B):
    return pl.ds(pl.multiple_of(i * size, size), size)


def kernel(
    act, gain, wq, wk, wv, wo, cos_all, sin_all, out,
    a1, a2, w, wkv, wout, stage1, stage2, got1, got2, own1, own2, kv_stage, kv_got, kv_own, kvo, inv, cos, sin, q,
    ss1, ss2,
    loc_sem, agy_s, agy_r, agz_s, agz_r, ss_s, ss_r, ssx_s, ssx_r, w_s, w_r, wf_s, wf_r, kvw_s, kvw_r, rs_s, rs_r, kvp_s, kvp_r, kvg_s,
    kvg_r, kvf_s, kvf_r,
):
    row, col = lax.axis_index("row"), lax.axis_index("col")
    yh, co = row // 2, row % 2
    z, yl, x = col // 8, (col // 4) % 2, col % 4
    g = z * 2 + yl

    def at(yh_, co_, z_, yl_, x_):
        return (yh_ * 2 + co_, z_ * 8 + yl_ * 4 + x_)

    z_peers = [at(yh, co, (z + d) % 4, yl, x) for d in (1, 3, 2)]
    yl_peer = at(yh, co, z, 1 - yl, x)
    x_at = [(x + d) % 4 for d in (1, 3, 2)]
    x_peers = [at(yh, co, z, yl, v) for v in x_at]
    y_peer = at(1 - yh, co, z, yl, x)
    sibling = at(yh, 1 - co, z, yl, x)

    barrier = pltpu.get_barrier_semaphore()
    everyone = z_peers + [yl_peer] + x_peers + [y_peer, sibling]
    for peer in everyone:
        pl.semaphore_signal(barrier, inc=1, device_id=peer, device_id_type=MESH)

    sent = []

    def send(src, dst, s, r, device):
        copy = remote(src, dst, s, r, device)
        copy.start()
        sent.append(copy)

    def arrived(dst, s, r):
        remote(dst, dst, s, r, sibling).wait_recv()

    local = [
        pltpu.make_async_copy(cos_all.at[block(row, TOK)], cos, loc_sem.at[0]),
        pltpu.make_async_copy(sin_all.at[block(row, TOK)], sin, loc_sem.at[1]),
        pltpu.make_async_copy(wk.at[:, x, :, block(g, 128)], wkv.at[pl.ds(2 * row, 2), :, pl.ds(0, 128)], loc_sem.at[2]),
        pltpu.make_async_copy(wv.at[:, x, :, block(g, 128)], wkv.at[pl.ds(2 * row, 2), :, pl.ds(128, 128)], loc_sem.at[3]),
        pltpu.make_async_copy(wq.at[:, x], w.at[pl.ds(2 * row, 2), :, block(x)], loc_sem.at[4]),
        pltpu.make_async_copy(wo.at[:, x], wout.at[pl.ds(2 * row, 2), :, block(x)], loc_sem.at[5]),
    ]
    for copy in local:
        copy.start()
    a1[:, block(g)] = (act[...].astype(F32) * gain[...].astype(F32).reshape(1, B)).astype(BF16)
    along = (((1,), (1,)), ((), ()))

    wide = act[...].astype(F32)
    square = wide * wide
    high = square.astype(BF16)
    low = (square - high.astype(F32)).astype(BF16)
    ones = jnp.ones((8, B), BF16)
    sums = lax.dot_general(ones, high, along, preferred_element_type=F32) + lax.dot_general(
        ones, low, along, preferred_element_type=F32
    )
    ss1[g] = sums[0:1]
    kvo[:, 2 * HEAD_DIM :] = jnp.ones((LENGTH, HEAD_DIM), BF16)

    pl.semaphore_wait(barrier, len(everyone))

    other = z * 2 + 1 - yl

    def tile(phase, a, t, who):
        size = HB if phase else B
        return a.at[pl.ds(t * size, size), block(who)]

    def half(phase, a, t, who, h):
        size = HB // 2 if phase else B // 2
        return a.at[pl.ds((2 * t + h) * size, size), block(who)]

    def gather_first(phase, a, t):
        send(tile(phase, a, t, g), tile(phase, a, t, g), agy_s.at[phase, t], agy_r.at[phase, t], yl_peer)

    def gather_spread(phase, a, t, who, slot):
        for d, h in ((0, 0), (1, 1), (0, 1), (1, 0)):
            piece = half(phase, a, t, who, h)
            send(piece, piece, agz_s.at[phase, t, slot, d * 2 + h], agz_r.at[phase, t, who, d * 2 + h], z_peers[d])

    def gather_second(phase, a, t):
        arrived(tile(phase, a, t, other), agy_s.at[phase, t], agy_r.at[phase, t])
        gather_spread(phase, a, t, other, 1)

    def gather_relay(phase, a, t, same):
        y = yl if same else 1 - yl
        for d, h, to in ((3, 0, 0), (1, 1, 1)):
            who = ((z + d) % 4) * 2 + y
            piece = half(phase, a, t, who, h)
            arrived(piece, agz_s.at[phase, t, 0, 0], agz_r.at[phase, t, who, to * 3])
            send(piece, piece, agz_s.at[phase, t, 2, to * 2 + int(same)], agz_r.at[phase, t, who, to * 3], z_peers[to])

    def gather_wait(phase, a, t):
        for y in range(2):
            for d, h, k in ((3, 1, 1), (1, 0, 2), (2, 0, 0), (2, 1, 3)):
                who = ((z + d) % 4) * 2 + y
                arrived(half(phase, a, t, who, h), agz_s.at[phase, t, 0, 0], agz_r.at[phase, t, who, k])

    far_row = (1 - yh) * 2 + co

    def weight_piece(dst, r, xs):
        return dst.at[pl.ds(2 * r, 2), :, block(xs)]

    def weight_first(phase, src, dst):
        for k, (xd, peer) in enumerate(zip(x_at, x_peers)):
            send(src.at[:, xd], weight_piece(dst, row, x), w_s.at[phase, k], w_r.at[phase, 0, x], peer)

    def weight_down(phase, src, dst):
        send(src.at[:, x], weight_piece(dst, row, x), w_s.at[phase, 3], w_r.at[phase, 1, x], y_peer)

    def weight_relay(phase, dst, k):
        piece = weight_piece(dst, row, x_at[k])
        arrived(piece, w_s.at[phase, 0], w_r.at[phase, 0, x_at[k]])
        send(piece, piece, w_s.at[phase, 4 + k], w_r.at[phase, 1, x_at[k]], y_peer)

    def weight_near(phase, dst):
        local[4 + phase].wait()
        slab = dst.at[pl.ds(2 * row, 2)]
        send(slab, slab, wf_s.at[phase, 0], wf_r.at[phase, 0], sibling)

    def weight_far(phase, dst, k):
        xs = ([x] + x_at)[k]
        piece = weight_piece(dst, far_row, xs)
        arrived(piece, w_s.at[phase, 0], w_r.at[phase, 1, xs])
        send(piece, piece, wf_s.at[phase, 1 + k], wf_r.at[phase, 1 + k], sibling)

    def weight_wait(phase, dst):
        arrived(dst.at[pl.ds(2 * (row + 1 - 2 * co), 2)], wf_s.at[phase, 0], wf_r.at[phase, 0])
        for k, xs in enumerate([x] + x_at):
            piece = weight_piece(dst, far_row + 1 - 2 * co, xs)
            arrived(piece, wf_s.at[phase, 1 + k], wf_r.at[phase, 1 + k])

    def kv_slab(r):
        return wkv.at[pl.ds(2 * r, 2)]

    def kv_weight_first():
        local[2].wait()
        local[3].wait()
        send(kv_slab(row), kv_slab(row), kvw_s.at[0], kvw_r.at[0], y_peer)
        send(kv_slab(row), kv_slab(row), kvw_s.at[1], kvw_r.at[1], sibling)

    def kv_weight_relay():
        arrived(kv_slab(far_row), kvw_s.at[0], kvw_r.at[0])
        send(kv_slab(far_row), kv_slab(far_row), kvw_s.at[2], kvw_r.at[2], sibling)

    def kv_weight_wait():
        arrived(kv_slab(row + 1 - 2 * co), kvw_s.at[1], kvw_r.at[1])
        arrived(kv_slab(far_row + 1 - 2 * co), kvw_s.at[2], kvw_r.at[2])

    def partial_one(a, weights, first, size, xd):
        return jnp.dot(
            a[pl.ds(first, size), :], weights[:, :, block(xd)].reshape(8 * B, B), preferred_element_type=F32
        )

    def partial_make(a, weights, stage, own, first, size):
        rows = pl.ds(first, size)
        for k, xd in enumerate(x_at):
            stage[k, rows, :] = partial_one(a, weights, first, size, xd).astype(BF16)
        own[rows, :] = partial_one(a, weights, first, size, x)

    def partial_start(phase, stage, got, u):
        rows = pl.ds(u * HB, HB)
        for k in (2, 0, 1):
            send(stage.at[k, rows], got.at[x, rows], rs_s.at[phase, u, k], rs_r.at[phase, u, x], x_peers[k])

    def partial_sum(phase, got, own, u):
        rows = pl.ds(u * HB, HB)
        total = own[rows, :]
        for xs in x_at:
            arrived(got.at[xs, rows], rs_s.at[phase, u, 0], rs_r.at[phase, u, xs])
            total = total + got[xs, rows, :].astype(F32)
        return total

    def squares_first():
        for k, peer in enumerate([yl_peer] + z_peers):
            send(ss1.at[g], ss1.at[g], ss_s.at[k], ss_r.at[g], peer)

    def squares_relay():
        arrived(ss1.at[other], ss_s.at[0], ss_r.at[other])
        for k, peer in enumerate(z_peers):
            send(ss1.at[other], ss1.at[other], ss_s.at[4 + k], ss_r.at[other], peer)

    def squares_second():
        for d in (1, 3, 2):
            for y in range(2):
                who = ((z + d) % 4) * 2 + y
                arrived(ss1.at[who], ss_s.at[0], ss_r.at[who])
        ss2[x] = jnp.sum(ss1[...], axis=0)
        for k, peer in enumerate(x_peers):
            send(ss2.at[x], ss2.at[x], ssx_s.at[k], ssx_r.at[x], peer)

    def squares_wait():
        for xs in x_at:
            arrived(ss2.at[xs], ssx_s.at[0], ssx_r.at[xs])
        factor = lax.rsqrt(jnp.sum(ss2[...], axis=0) / D + 1e-05)
        for b in range(TOK // 128):
            inv[pl.ds(b * 128, 128), :] = jnp.broadcast_to(factor[:, b * 128 : (b + 1) * 128], (128, 128)).T

    above = row - 2

    def kv_part(t):
        rows = pl.ds(t * B, B)
        part = jnp.dot(a1[rows, :], wkv[...].reshape(8 * B, B), preferred_element_type=F32)
        kv_stage[rows, :] = part.astype(BF16)
        kv_own[t] = part
        for k, xd in enumerate(x_at):
            piece = kv_stage.at[pl.ds(pl.multiple_of(t * B + xd * SUB, SUB), SUB)]
            send(piece, kv_got.at[t, x], kvp_s.at[t, k], kvp_r.at[t, x], x_peers[k])

    def kv_piece(r, t, xs):
        return kvo.at[pl.ds(pl.multiple_of(r * TOK + t * B + xs * SUB, SUB), SUB), pl.ds(0, 2 * HEAD_DIM)]

    def kv_down(t):
        return remote(kv_piece(row, t, x), kv_piece(row, t, x), kvg_s.at[t, 3], kvg_r.at[1, t, x], y_peer)

    def kv_reduce(t):
        total = kv_own[t, block(x, SUB), :]
        for k, xs in enumerate(x_at):
            arrived(kv_got.at[t, xs], kvp_s.at[t, k], kvp_r.at[t, xs])
            total = total + kv_got[t, xs].astype(F32)
        mine = pl.ds(pl.multiple_of(t * B + x * SUB, SUB), SUB)
        scale = inv[mine, :]
        key = total[:, :HEAD_DIM] * scale
        key = (key * cos[mine, :] + pltpu.roll(key, HEAD_DIM // 2, 1) * sin[mine, :]).astype(BF16)
        value = (total[:, HEAD_DIM:] * scale).astype(BF16)
        kvo[pl.ds(pl.multiple_of(row * TOK + t * B + x * SUB, SUB), SUB), 0 : 2 * HEAD_DIM] = jnp.concatenate(
            [key, value], axis=1
        )

        @pl.when(yh == 0)
        def _():
            kv_down(t).start()

        for k, peer in enumerate(x_peers):
            send(kv_piece(row, t, x), kv_piece(row, t, x), kvg_s.at[t, k], kvg_r.at[0, t, x], peer)

    def kv_relay_copies(t):
        piece = kv_piece(above, t, x)
        return [remote(piece, piece, kvg_s.at[t, 4 + k], kvg_r.at[1, t, x], peer) for k, peer in enumerate(x_peers)]

    def kv_relay(t):
        @pl.when(yh == 1)
        def _():
            arrived(kv_piece(above, t, x), kvg_s.at[t, 0], kvg_r.at[1, t, x])
            for copy in kv_relay_copies(t):
                copy.start()

    def kv_whole(r):
        return kvo.at[block(r, TOK), pl.ds(0, 2 * HEAD_DIM)]

    def kv_across(which, r):
        return remote(kv_whole(r), kv_whole(r), kvf_s.at[which], kvf_r.at[which], sibling)

    def kv_own_wait():
        for t in range(CHUNKS):
            for xs in x_at:
                arrived(kv_piece(row, t, xs), kvg_s.at[t, 0], kvg_r.at[0, t, xs])

        @pl.when(co == 0)
        def _():
            kv_across(0, row).start()

    def kv_rest_wait():
        @pl.when(yh == 1)
        def _():
            for t in range(CHUNKS):
                for xs in x_at:
                    arrived(kv_piece(above, t, xs), kvg_s.at[t, 0], kvg_r.at[1, t, xs])
            kv_across(1, above).start()
            arrived(kv_whole(above + 1 - 2 * co), kvf_s.at[1], kvf_r.at[1])

        @pl.when(co == 1)
        def _():
            arrived(kv_whole(row - 1), kvf_s.at[0], kvf_r.at[0])

    gather_first(0, a1, 0)
    squares_first()
    gather_spread(0, a1, 0, g, 0)
    gather_first(0, a1, 1)
    gather_spread(0, a1, 1, g, 0)
    weight_first(0, wq, w)
    kv_weight_first()
    gather_first(0, a1, 2)
    gather_first(0, a1, 3)
    weight_down(0, wq, w)
    weight_first(1, wo, wout)

    def gather_turn(phase, a, t):
        gather_second(phase, a, t)
        gather_relay(phase, a, t, True)
        gather_relay(phase, a, t, False)

    gather_second(0, a1, 0)
    squares_relay()
    gather_relay(0, a1, 0, True)
    gather_relay(0, a1, 0, False)
    gather_spread(0, a1, 2, g, 0)
    weight_relay(0, w, 0)
    weight_relay(0, w, 1)

    gather_turn(0, a1, 1)
    gather_spread(0, a1, 3, g, 0)
    kv_weight_relay()
    weight_relay(0, w, 2)
    weight_near(0, w)
    squares_second()

    gather_second(0, a1, 2)
    gather_relay(0, a1, 2, True)
    kv_weight_wait()
    gather_wait(0, a1, 0)
    kv_part(0)
    gather_relay(0, a1, 2, False)

    gather_second(0, a1, 3)
    gather_relay(0, a1, 3, True)
    gather_wait(0, a1, 1)
    kv_part(1)
    local[0].wait()
    local[1].wait()
    squares_wait()
    kv_reduce(0)
    gather_relay(0, a1, 3, False)

    gather_wait(0, a1, 2)
    kv_part(2)
    kv_reduce(1)
    for k in range(3):
        weight_far(0, w, k)
    gather_wait(0, a1, 3)
    kv_part(3)
    kv_reduce(2)
    kv_reduce(3)
    for t in range(3):
        kv_relay(t)

    weight_down(1, wo, wout)
    weight_relay(1, wout, 0)
    weight_relay(1, wout, 1)
    weight_far(0, w, 3)
    weight_wait(0, w)
    partial_make(a1, w, stage1, own1, 0, B)
    partial_start(0, stage1, got1, 0)
    kv_relay(3)
    partial_make(a1, w, stage1, own1, B, B)
    kv_own_wait()
    partial_start(0, stage1, got1, 1)
    partial_make(a1, w, stage1, own1, 2 * B, B)
    partial_make(a1, w, stage1, own1, 3 * B, B)
    partial_start(0, stage1, got1, 2)

    def query_ready(u, n):
        for v in range(n):
            rows = pl.ds((u + v) * HB, HB)
            total = partial_sum(0, got1, own1, u + v)
            scale = inv[rows, :] * SCALE
            for h in range(2):
                part = total[:, h * HEAD_DIM : (h + 1) * HEAD_DIM] * scale
                part = part * cos[rows, :] + pltpu.roll(part, HEAD_DIM // 2, 1) * sin[rows, :]
                q[pl.ds((h * n + v) * HB, HB), :] = part.astype(BF16)

    def attend(u, n):
        count = n * HB
        width = (u + n) * HB
        queries = pl.ds(0, 2 * count)
        here = kvo[pl.ds(pl.multiple_of(row * TOK, TOK), width), :]
        s = lax.dot_general(q[queries, :], here[:, :HEAD_DIM], along, preferred_element_type=F32)
        query_at = lax.broadcasted_iota(jnp.int32, s.shape, 0) % count + u * HB
        key_at = lax.broadcasted_iota(jnp.int32, s.shape, 1)
        s = jnp.where(key_at <= query_at, s, -1e30)
        top = jnp.max(s, axis=1, keepdims=True)
        p = jnp.exp2(s - top).astype(BF16)
        acc = jnp.dot(p, here[:, HEAD_DIM:], preferred_element_type=F32)
        if u == 0:
            kv_rest_wait()

        def step(kb, carry):
            top, acc = carry
            there = kvo[block(kb, TOK), :]
            s = lax.dot_general(q[queries, :], there[:, :HEAD_DIM], along, preferred_element_type=F32)
            new = jnp.maximum(top, jnp.max(s, axis=1, keepdims=True))
            p = jnp.exp2(s - new).astype(BF16)
            acc = acc * jnp.exp2(top - new) + jnp.dot(p, there[:, HEAD_DIM:], preferred_element_type=F32)
            return new, acc

        top, acc = lax.fori_loop(0, row, step, (top, acc))
        mixed = (acc[:, :HEAD_DIM] / acc[:, HEAD_DIM:]).astype(BF16)
        a2[pl.ds(u * HB, count), block(g)] = jnp.concatenate([mixed[:count], mixed[count:]], axis=1)

    def out_part(u):
        gather_wait(1, a2, u)
        partial_make(a2, wout, stage2, own2, u * HB, HB)
        partial_start(1, stage2, got2, u)

    def out_sum(u):
        out[pl.ds(u * HB, HB), :] = partial_sum(1, got2, own2, u).astype(BF16)

    def turn_out(u):
        gather_first(1, a2, u)
        gather_spread(1, a2, u, g, 0)

    def turn_second(u):
        gather_second(1, a2, u)
        gather_relay(1, a2, u, True)

    query_ready(0, 1)
    attend(0, 1)
    turn_out(0)
    partial_start(0, stage1, got1, 3)
    weight_relay(1, wout, 2)
    weight_near(1, wout)

    query_ready(1, 1)
    attend(1, 1)
    turn_out(1)
    partial_start(0, stage1, got1, 4)
    partial_start(0, stage1, got1, 5)

    query_ready(2, 2)
    attend(2, 2)
    turn_out(2)
    turn_out(3)
    partial_start(0, stage1, got1, 6)
    partial_start(0, stage1, got1, 7)
    turn_second(0)
    turn_second(1)
    weight_far(1, wout, 0)
    weight_far(1, wout, 1)
    weight_far(1, wout, 2)

    query_ready(4, 2)
    attend(4, 2)
    turn_out(4)
    turn_out(5)
    gather_relay(1, a2, 0, False)
    gather_relay(1, a2, 1, False)
    turn_second(2)
    turn_second(3)
    weight_far(1, wout, 3)

    query_ready(6, 2)
    attend(6, 2)
    turn_out(6)
    turn_out(7)
    weight_wait(1, wout)
    gather_relay(1, a2, 2, False)
    out_part(0)
    gather_relay(1, a2, 3, False)
    turn_second(4)
    out_part(1)
    turn_second(5)
    out_part(2)
    turn_second(6)
    gather_relay(1, a2, 4, False)
    out_part(3)
    turn_second(7)
    gather_relay(1, a2, 5, False)
    out_sum(0)
    out_part(4)
    gather_relay(1, a2, 6, False)
    out_sum(1)
    out_part(5)
    gather_relay(1, a2, 7, False)
    out_sum(2)
    out_part(6)
    out_sum(3)
    out_part(7)
    for u in range(4, TURNS):
        out_sum(u)

    for copy in sent:
        copy.wait_send()

    @pl.when(yh == 0)
    def _():
        for t in range(CHUNKS):
            kv_down(t).wait_send()

    @pl.when(yh == 1)
    def _():
        for t in range(CHUNKS):
            for copy in kv_relay_copies(t):
                copy.wait_send()
        kv_across(1, above).wait_send()

    @pl.when(co == 0)
    def _():
        kv_across(0, row).wait_send()


def local_step(activations, norm_gain, w_query, w_key, w_value, w_out):
    cos, sin = rope_constants()
    dma = pltpu.SemaphoreType.DMA
    vmem = pl.BlockSpec(memory_space=pltpu.VMEM)
    hbm = pl.BlockSpec(memory_space=pl.ANY)
    return pl.pallas_call(
        kernel,
        out_shape=jax.ShapeDtypeStruct((TOK, B), BF16),
        in_specs=[vmem, vmem] + [hbm] * 6,
        out_specs=vmem,
        scratch_shapes=[
            pltpu.VMEM((TOK, 8 * B), BF16),
            pltpu.VMEM((TOK, 8 * B), BF16),
            pltpu.VMEM((8, B, 4 * B), BF16),
            pltpu.VMEM((8, B, B), BF16),
            pltpu.VMEM((8, B, 4 * B), BF16),
            pltpu.VMEM((3, TOK, B), BF16),
            pltpu.VMEM((3, TOK, B), BF16),
            pltpu.VMEM((4, TOK, B), BF16),
            pltpu.VMEM((4, TOK, B), BF16),
            pltpu.VMEM((TOK, B), F32),
            pltpu.VMEM((TOK, B), F32),
            pltpu.VMEM((TOK, B), BF16),
            pltpu.VMEM((CHUNKS, 4, SUB, B), BF16),
            pltpu.VMEM((CHUNKS, B, B), F32),
            pltpu.VMEM((LENGTH, 3 * HEAD_DIM), BF16),
            pltpu.VMEM((TOK, 128), F32),
            pltpu.VMEM((TOK, HEAD_DIM), F32),
            pltpu.VMEM((TOK, HEAD_DIM), F32),
            pltpu.VMEM((4 * HB, HEAD_DIM), BF16),
            pltpu.VMEM((8, 1, TOK), F32),
            pltpu.VMEM((4, 1, TOK), F32),
            dma((6,)),
            dma((2, TURNS)),
            dma((2, TURNS)),
            dma((2, TURNS, 3, 4)),
            dma((2, TURNS, 8, 4)),
            dma((8,)),
            dma((8,)),
            dma((4,)),
            dma((4,)),
            dma((2, 8)),
            dma((2, 2, 4)),
            dma((2, 5)),
            dma((2, 5)),
            dma((3,)),
            dma((3,)),
            dma((2, TURNS, 4)),
            dma((2, TURNS, 4)),
            dma((CHUNKS, 4)),
            dma((CHUNKS, 4)),
            dma((CHUNKS, 8)),
            dma((2, CHUNKS, 4)),
            dma((2,)),
            dma((2,)),
        ],
        compiler_params=pltpu.CompilerParams(
            collective_id=0, has_side_effects=True, vmem_limit_bytes=58 * 2**20
        ),
    )(
        activations,
        norm_gain,
        w_query.reshape(2, 4, B, B),
        w_key.reshape(2, 4, B, 1024),
        w_value.reshape(2, 4, B, 1024),
        w_out.reshape(2, 4, B, B),
        cos,
        sin,
    )


def solution(mesh):
    placed = (
        P("row", "col"),
        P("col"),
        P("row", "col"),
        P("row", None),
        P("row", None),
        P("row", "col"),
    )
    return jax.shard_map(
        local_step, mesh=mesh, in_specs=placed, out_specs=P("row", "col"), check_vma=False
    )
```

```python
import functools

import jax
import jax.numpy as jnp
import numpy as np
from jax import lax
from jax.experimental import pallas as pl
from jax.experimental.pallas import tpu as pltpu
from jax.sharding import PartitionSpec as P

MESH = pl.DeviceIdType.MESH
HEAD_DIM = 128
TOK = 1024
B = 256
CHUNKS = TOK // B
HB = B // 2
TURNS = TOK // HB
SUB = B // 4
LENGTH = 4096
D = 8192
SCALE = HEAD_DIM**-0.5 * 1.4426950408889634
F32 = jnp.float32
BF16 = jnp.bfloat16


def rope_constants():
    half = HEAD_DIM // 2
    frequency = np.exp(-np.log(500000.0) * (np.arange(half) * (2.0 / HEAD_DIM)))
    angles = np.arange(LENGTH)[:, None] * frequency[None, :]
    cos, sin = np.cos(angles), np.sin(angles)
    return (
        np.concatenate([cos, cos], 1).astype(np.float32),
        np.concatenate([-sin, sin], 1).astype(np.float32),
    )


def remote(src, dst, send, recv, device):
    return pltpu.make_async_remote_copy(
        src_ref=src, dst_ref=dst, send_sem=send, recv_sem=recv, device_id=device, device_id_type=MESH
    )


def block(i, size=B):
    return pl.ds(pl.multiple_of(i * size, size), size)


def kernel(
    act, gain, wq, wk, wv, wo, cos_all, sin_all, out,
    a1, a2, w, wkv, wout, stage1, stage2, got1, got2, own1, own2, kv_stage, kv_got, kv_own, kvo, inv, cos, sin, q,
    ss1, ss2,
    loc_sem, agy_s, agy_r, agz_s, agz_r, ss_s, ss_r, ssx_s, ssx_r, w_s, w_r, wf_s, wf_r, kvw_s, kvw_r, rs_s, rs_r, kvp_s, kvp_r, kvg_s,
    kvg_r, kvf_s, kvf_r,
):
    row, col = lax.axis_index("row"), lax.axis_index("col")
    yh, co = row // 2, row % 2
    z, yl, x = col // 8, (col // 4) % 2, col % 4
    g = z * 2 + yl

    def at(yh_, co_, z_, yl_, x_):
        return (yh_ * 2 + co_, z_ * 8 + yl_ * 4 + x_)

    z_peers = [at(yh, co, (z + d) % 4, yl, x) for d in (1, 3, 2)]
    yl_peer = at(yh, co, z, 1 - yl, x)
    x_at = [(x + d) % 4 for d in (1, 3, 2)]
    x_peers = [at(yh, co, z, yl, v) for v in x_at]
    y_peer = at(1 - yh, co, z, yl, x)
    sibling = at(yh, 1 - co, z, yl, x)

    barrier = pltpu.get_barrier_semaphore()
    everyone = z_peers + [yl_peer] + x_peers + [y_peer, sibling]
    for peer in everyone:
        pl.semaphore_signal(barrier, inc=1, device_id=peer, device_id_type=MESH)

    sent = []

    def send(src, dst, s, r, device):
        copy = remote(src, dst, s, r, device)
        copy.start()
        sent.append(copy)

    def arrived(dst, s, r):
        remote(dst, dst, s, r, sibling).wait_recv()

    local = [
        pltpu.make_async_copy(cos_all.at[block(row, TOK)], cos, loc_sem.at[0]),
        pltpu.make_async_copy(sin_all.at[block(row, TOK)], sin, loc_sem.at[1]),
        pltpu.make_async_copy(wk.at[:, x, :, block(g, 128)], wkv.at[pl.ds(2 * row, 2), :, pl.ds(0, 128)], loc_sem.at[2]),
        pltpu.make_async_copy(wv.at[:, x, :, block(g, 128)], wkv.at[pl.ds(2 * row, 2), :, pl.ds(128, 128)], loc_sem.at[3]),
        pltpu.make_async_copy(wq.at[:, x], w.at[pl.ds(2 * row, 2), :, block(x)], loc_sem.at[4]),
        pltpu.make_async_copy(wo.at[:, x], wout.at[pl.ds(2 * row, 2), :, block(x)], loc_sem.at[5]),
    ]
    for copy in local:
        copy.start()
    a1[:, block(g)] = (act[...].astype(F32) * gain[...].astype(F32).reshape(1, B)).astype(BF16)
    along = (((1,), (1,)), ((), ()))

    wide = act[...].astype(F32)
    square = wide * wide
    high = square.astype(BF16)
    low = (square - high.astype(F32)).astype(BF16)
    ones = jnp.ones((8, B), BF16)
    sums = lax.dot_general(ones, high, along, preferred_element_type=F32) + lax.dot_general(
        ones, low, along, preferred_element_type=F32
    )
    ss1[g] = sums[0:1]
    kvo[:, 2 * HEAD_DIM :] = jnp.ones((LENGTH, HEAD_DIM), BF16)

    pl.semaphore_wait(barrier, len(everyone))

    other = z * 2 + 1 - yl

    def tile(phase, a, t, who):
        size = HB if phase else B
        return a.at[pl.ds(t * size, size), block(who)]

    def gather_first(phase, a, t):
        send(tile(phase, a, t, g), tile(phase, a, t, g), agy_s.at[phase, t], agy_r.at[phase, t], yl_peer)

    def gather_spread(phase, a, t, who, slot):
        piece = tile(phase, a, t, who)
        for d in (0, 1) if t % 2 == 0 else (1, 0):
            send(piece, piece, agz_s.at[phase, t, slot, d], agz_r.at[phase, t, who, d], z_peers[d])

    def gather_second(phase, a, t):
        arrived(tile(phase, a, t, other), agy_s.at[phase, t], agy_r.at[phase, t])
        gather_spread(phase, a, t, other, 1)

    def gather_relay(phase, a, t, same):
        y = yl if same else 1 - yl
        to = t % 2
        who = ((z + (3, 1)[to]) % 4) * 2 + y
        piece = tile(phase, a, t, who)
        arrived(piece, agz_s.at[phase, t, 0, 0], agz_r.at[phase, t, who, to])
        send(piece, piece, agz_s.at[phase, t, 2, int(same)], agz_r.at[phase, t, who, to], z_peers[to])

    def gather_wait(phase, a, t):
        to = t % 2
        for y in range(2):
            for d, k in (((1, 1), (2, 0)) if to == 0 else ((3, 0), (2, 1))):
                who = ((z + d) % 4) * 2 + y
                arrived(tile(phase, a, t, who), agz_s.at[phase, t, 0, 0], agz_r.at[phase, t, who, k])

    far_row = (1 - yh) * 2 + co

    def weight_piece(dst, r, xs):
        return dst.at[pl.ds(2 * r, 2), :, block(xs)]

    def weight_first(phase, src, dst):
        for k, (xd, peer) in enumerate(zip(x_at, x_peers)):
            send(src.at[:, xd], weight_piece(dst, row, x), w_s.at[phase, k], w_r.at[phase, 0, x], peer)

    def weight_down(phase, src, dst):
        send(src.at[:, x], weight_piece(dst, row, x), w_s.at[phase, 3], w_r.at[phase, 1, x], y_peer)

    def weight_relay(phase, dst, k):
        piece = weight_piece(dst, row, x_at[k])
        arrived(piece, w_s.at[phase, 0], w_r.at[phase, 0, x_at[k]])
        send(piece, piece, w_s.at[phase, 4 + k], w_r.at[phase, 1, x_at[k]], y_peer)

    def weight_near(phase, dst):
        local[4 + phase].wait()
        slab = dst.at[pl.ds(2 * row, 2)]
        send(slab, slab, wf_s.at[phase, 0], wf_r.at[phase, 0], sibling)

    def weight_far(phase, dst, k):
        xs = ([x] + x_at)[k]
        piece = weight_piece(dst, far_row, xs)
        arrived(piece, w_s.at[phase, 0], w_r.at[phase, 1, xs])
        send(piece, piece, wf_s.at[phase, 1 + k], wf_r.at[phase, 1 + k], sibling)

    def weight_wait(phase, dst):
        arrived(dst.at[pl.ds(2 * (row + 1 - 2 * co), 2)], wf_s.at[phase, 0], wf_r.at[phase, 0])
        for k, xs in enumerate([x] + x_at):
            piece = weight_piece(dst, far_row + 1 - 2 * co, xs)
            arrived(piece, wf_s.at[phase, 1 + k], wf_r.at[phase, 1 + k])

    def kv_slab(r):
        return wkv.at[pl.ds(2 * r, 2)]

    def kv_weight_first():
        local[2].wait()
        local[3].wait()
        send(kv_slab(row), kv_slab(row), kvw_s.at[0], kvw_r.at[0], y_peer)
        send(kv_slab(row), kv_slab(row), kvw_s.at[1], kvw_r.at[1], sibling)

    def kv_weight_relay():
        arrived(kv_slab(far_row), kvw_s.at[0], kvw_r.at[0])
        send(kv_slab(far_row), kv_slab(far_row), kvw_s.at[2], kvw_r.at[2], sibling)

    def kv_weight_wait():
        arrived(kv_slab(row + 1 - 2 * co), kvw_s.at[1], kvw_r.at[1])
        arrived(kv_slab(far_row + 1 - 2 * co), kvw_s.at[2], kvw_r.at[2])

    def partial_one(a, weights, first, size, xd):
        return jnp.dot(
            a[pl.ds(first, size), :], weights[:, :, block(xd)].reshape(8 * B, B), preferred_element_type=F32
        )

    def partial_make(a, weights, stage, own, first, size):
        rows = pl.ds(first, size)
        for k, xd in enumerate(x_at):
            stage[k, rows, :] = partial_one(a, weights, first, size, xd).astype(BF16)
        own[rows, :] = partial_one(a, weights, first, size, x)

    def partial_start(phase, stage, got, u):
        rows = pl.ds(u * HB, HB)
        for k in (2, 0, 1):
            send(stage.at[k, rows], got.at[x, rows], rs_s.at[phase, u, k], rs_r.at[phase, u, x], x_peers[k])

    def partial_sum(phase, got, own, u):
        rows = pl.ds(u * HB, HB)
        total = own[rows, :]
        for xs in x_at:
            arrived(got.at[xs, rows], rs_s.at[phase, u, 0], rs_r.at[phase, u, xs])
            total = total + got[xs, rows, :].astype(F32)
        return total

    def squares_first():
        for k, peer in enumerate([yl_peer] + z_peers):
            send(ss1.at[g], ss1.at[g], ss_s.at[k], ss_r.at[g], peer)

    def squares_relay():
        arrived(ss1.at[other], ss_s.at[0], ss_r.at[other])
        for k, peer in enumerate(z_peers):
            send(ss1.at[other], ss1.at[other], ss_s.at[4 + k], ss_r.at[other], peer)

    def squares_second():
        for d in (1, 3, 2):
            for y in range(2):
                who = ((z + d) % 4) * 2 + y
                arrived(ss1.at[who], ss_s.at[0], ss_r.at[who])
        ss2[x] = jnp.sum(ss1[...], axis=0)
        for k, peer in enumerate(x_peers):
            send(ss2.at[x], ss2.at[x], ssx_s.at[k], ssx_r.at[x], peer)

    def squares_wait():
        for xs in x_at:
            arrived(ss2.at[xs], ssx_s.at[0], ssx_r.at[xs])
        factor = lax.rsqrt(jnp.sum(ss2[...], axis=0) / D + 1e-05)
        for b in range(TOK // 128):
            inv[pl.ds(b * 128, 128), :] = jnp.broadcast_to(factor[:, b * 128 : (b + 1) * 128], (128, 128)).T

    above = row - 2

    def kv_part(t):
        rows = pl.ds(t * B, B)
        part = jnp.dot(a1[rows, :], wkv[...].reshape(8 * B, B), preferred_element_type=F32)
        kv_stage[rows, :] = part.astype(BF16)
        kv_own[t] = part
        for k, xd in enumerate(x_at):
            piece = kv_stage.at[pl.ds(pl.multiple_of(t * B + xd * SUB, SUB), SUB)]
            send(piece, kv_got.at[t, x], kvp_s.at[t, k], kvp_r.at[t, x], x_peers[k])

    def kv_piece(r, t, xs):
        return kvo.at[pl.ds(pl.multiple_of(r * TOK + t * B + xs * SUB, SUB), SUB), pl.ds(0, 2 * HEAD_DIM)]

    def kv_down(t):
        return remote(kv_piece(row, t, x), kv_piece(row, t, x), kvg_s.at[t, 3], kvg_r.at[1, t, x], y_peer)

    def kv_reduce(t):
        total = kv_own[t, block(x, SUB), :]
        for k, xs in enumerate(x_at):
            arrived(kv_got.at[t, xs], kvp_s.at[t, k], kvp_r.at[t, xs])
            total = total + kv_got[t, xs].astype(F32)
        mine = pl.ds(pl.multiple_of(t * B + x * SUB, SUB), SUB)
        scale = inv[mine, :]
        key = total[:, :HEAD_DIM] * scale
        key = (key * cos[mine, :] + pltpu.roll(key, HEAD_DIM // 2, 1) * sin[mine, :]).astype(BF16)
        value = (total[:, HEAD_DIM:] * scale).astype(BF16)
        kvo[pl.ds(pl.multiple_of(row * TOK + t * B + x * SUB, SUB), SUB), 0 : 2 * HEAD_DIM] = jnp.concatenate(
            [key, value], axis=1
        )

        @pl.when(yh == 0)
        def _():
            kv_down(t).start()

        for k, peer in enumerate(x_peers):
            send(kv_piece(row, t, x), kv_piece(row, t, x), kvg_s.at[t, k], kvg_r.at[0, t, x], peer)

    def kv_relay_copies(t):
        piece = kv_piece(above, t, x)
        return [remote(piece, piece, kvg_s.at[t, 4 + k], kvg_r.at[1, t, x], peer) for k, peer in enumerate(x_peers)]

    def kv_relay(t):
        @pl.when(yh == 1)
        def _():
            arrived(kv_piece(above, t, x), kvg_s.at[t, 0], kvg_r.at[1, t, x])
            for copy in kv_relay_copies(t):
                copy.start()

    def kv_whole(r):
        return kvo.at[block(r, TOK), pl.ds(0, 2 * HEAD_DIM)]

    def kv_across(which, r):
        return remote(kv_whole(r), kv_whole(r), kvf_s.at[which], kvf_r.at[which], sibling)

    def kv_own_wait():
        for t in range(CHUNKS):
            for xs in x_at:
                arrived(kv_piece(row, t, xs), kvg_s.at[t, 0], kvg_r.at[0, t, xs])

        @pl.when(co == 0)
        def _():
            kv_across(0, row).start()

    def kv_rest_wait():
        @pl.when(yh == 1)
        def _():
            for t in range(CHUNKS):
                for xs in x_at:
                    arrived(kv_piece(above, t, xs), kvg_s.at[t, 0], kvg_r.at[1, t, xs])
            kv_across(1, above).start()
            arrived(kv_whole(above + 1 - 2 * co), kvf_s.at[1], kvf_r.at[1])

        @pl.when(co == 1)
        def _():
            arrived(kv_whole(row - 1), kvf_s.at[0], kvf_r.at[0])

    gather_first(0, a1, 0)
    squares_first()
    gather_spread(0, a1, 0, g, 0)
    gather_first(0, a1, 1)
    gather_spread(0, a1, 1, g, 0)
    weight_first(0, wq, w)
    kv_weight_first()
    gather_first(0, a1, 2)
    gather_first(0, a1, 3)
    weight_down(0, wq, w)
    weight_first(1, wo, wout)

    def gather_turn(phase, a, t):
        gather_second(phase, a, t)
        gather_relay(phase, a, t, True)
        gather_relay(phase, a, t, False)

    gather_second(0, a1, 0)
    squares_relay()
    gather_relay(0, a1, 0, True)
    gather_relay(0, a1, 0, False)
    gather_spread(0, a1, 2, g, 0)
    weight_relay(0, w, 0)
    weight_relay(0, w, 1)

    gather_turn(0, a1, 1)
    gather_spread(0, a1, 3, g, 0)
    kv_weight_relay()
    weight_relay(0, w, 2)
    weight_near(0, w)
    squares_second()

    gather_second(0, a1, 2)
    gather_relay(0, a1, 2, True)
    kv_weight_wait()
    gather_wait(0, a1, 0)
    kv_part(0)
    gather_relay(0, a1, 2, False)

    gather_second(0, a1, 3)
    gather_relay(0, a1, 3, True)
    gather_wait(0, a1, 1)
    kv_part(1)
    local[0].wait()
    local[1].wait()
    squares_wait()
    kv_reduce(0)
    gather_relay(0, a1, 3, False)

    gather_wait(0, a1, 2)
    kv_part(2)
    kv_reduce(1)
    for k in range(3):
        weight_far(0, w, k)
    gather_wait(0, a1, 3)
    kv_part(3)
    kv_reduce(2)
    kv_reduce(3)
    for t in range(3):
        kv_relay(t)

    weight_down(1, wo, wout)
    weight_relay(1, wout, 0)
    weight_relay(1, wout, 1)
    weight_far(0, w, 3)
    weight_wait(0, w)
    partial_make(a1, w, stage1, own1, 0, B)
    partial_start(0, stage1, got1, 0)
    kv_relay(3)
    partial_make(a1, w, stage1, own1, B, B)
    kv_own_wait()
    partial_start(0, stage1, got1, 1)
    partial_make(a1, w, stage1, own1, 2 * B, B)
    partial_make(a1, w, stage1, own1, 3 * B, B)
    partial_start(0, stage1, got1, 2)

    def query_ready(u, n):
        for v in range(n):
            rows = pl.ds((u + v) * HB, HB)
            total = partial_sum(0, got1, own1, u + v)
            scale = inv[rows, :] * SCALE
            for h in range(2):
                part = total[:, h * HEAD_DIM : (h + 1) * HEAD_DIM] * scale
                part = part * cos[rows, :] + pltpu.roll(part, HEAD_DIM // 2, 1) * sin[rows, :]
                q[pl.ds((h * n + v) * HB, HB), :] = part.astype(BF16)

    def attend(u, n):
        count = n * HB
        width = (u + n) * HB
        queries = pl.ds(0, 2 * count)
        here = kvo[pl.ds(pl.multiple_of(row * TOK, TOK), width), :]
        s = lax.dot_general(q[queries, :], here[:, :HEAD_DIM], along, preferred_element_type=F32)
        query_at = lax.broadcasted_iota(jnp.int32, s.shape, 0) % count + u * HB
        key_at = lax.broadcasted_iota(jnp.int32, s.shape, 1)
        s = jnp.where(key_at <= query_at, s, -1e30)
        top = jnp.max(s, axis=1, keepdims=True)
        p = jnp.exp2(s - top).astype(BF16)
        acc = jnp.dot(p, here[:, HEAD_DIM:], preferred_element_type=F32)
        if u == 0:
            kv_rest_wait()

        def step(kb, carry):
            top, acc = carry
            there = kvo[block(kb, TOK), :]
            s = lax.dot_general(q[queries, :], there[:, :HEAD_DIM], along, preferred_element_type=F32)
            new = jnp.maximum(top, jnp.max(s, axis=1, keepdims=True))
            p = jnp.exp2(s - new).astype(BF16)
            acc = acc * jnp.exp2(top - new) + jnp.dot(p, there[:, HEAD_DIM:], preferred_element_type=F32)
            return new, acc

        top, acc = lax.fori_loop(0, row, step, (top, acc))
        mixed = (acc[:, :HEAD_DIM] / acc[:, HEAD_DIM:]).astype(BF16)
        a2[pl.ds(u * HB, count), block(g)] = jnp.concatenate([mixed[:count], mixed[count:]], axis=1)

    def out_part(u):
        gather_wait(1, a2, u)
        partial_make(a2, wout, stage2, own2, u * HB, HB)
        partial_start(1, stage2, got2, u)

    def out_sum(u):
        out[pl.ds(u * HB, HB), :] = partial_sum(1, got2, own2, u).astype(BF16)

    def turn_out(u):
        gather_first(1, a2, u)
        gather_spread(1, a2, u, g, 0)

    def turn_second(u):
        gather_second(1, a2, u)
        gather_relay(1, a2, u, True)

    query_ready(0, 1)
    attend(0, 1)
    turn_out(0)
    partial_start(0, stage1, got1, 3)
    weight_relay(1, wout, 2)
    weight_near(1, wout)

    query_ready(1, 1)
    attend(1, 1)
    turn_out(1)
    partial_start(0, stage1, got1, 4)
    partial_start(0, stage1, got1, 5)

    query_ready(2, 2)
    attend(2, 2)
    turn_out(2)
    turn_out(3)
    partial_start(0, stage1, got1, 6)
    partial_start(0, stage1, got1, 7)
    turn_second(0)
    turn_second(1)
    weight_far(1, wout, 0)
    weight_far(1, wout, 1)
    weight_far(1, wout, 2)

    query_ready(4, 2)
    attend(4, 2)
    turn_out(4)
    turn_out(5)
    gather_relay(1, a2, 0, False)
    gather_relay(1, a2, 1, False)
    turn_second(2)
    turn_second(3)
    weight_far(1, wout, 3)

    query_ready(6, 2)
    attend(6, 2)
    turn_out(6)
    turn_out(7)
    turn_second(4)
    weight_wait(1, wout)
    gather_relay(1, a2, 2, False)
    out_part(0)
    gather_relay(1, a2, 3, False)
    turn_second(5)
    out_part(1)
    gather_relay(1, a2, 4, False)
    turn_second(6)
    out_part(2)
    gather_relay(1, a2, 5, False)
    turn_second(7)
    out_part(3)
    out_sum(0)
    gather_relay(1, a2, 6, False)
    out_part(4)
    out_sum(1)
    gather_relay(1, a2, 7, False)
    out_part(5)
    out_sum(2)
    out_part(6)
    out_sum(3)
    out_part(7)
    for u in range(4, TURNS):
        out_sum(u)

    for copy in sent:
        copy.wait_send()

    @pl.when(yh == 0)
    def _():
        for t in range(CHUNKS):
            kv_down(t).wait_send()

    @pl.when(yh == 1)
    def _():
        for t in range(CHUNKS):
            for copy in kv_relay_copies(t):
                copy.wait_send()
        kv_across(1, above).wait_send()

    @pl.when(co == 0)
    def _():
        kv_across(0, row).wait_send()


def local_step(activations, norm_gain, w_query, w_key, w_value, w_out):
    cos, sin = rope_constants()
    dma = pltpu.SemaphoreType.DMA
    vmem = pl.BlockSpec(memory_space=pltpu.VMEM)
    hbm = pl.BlockSpec(memory_space=pl.ANY)
    return pl.pallas_call(
        kernel,
        out_shape=jax.ShapeDtypeStruct((TOK, B), BF16),
        in_specs=[vmem, vmem] + [hbm] * 6,
        out_specs=vmem,
        scratch_shapes=[
            pltpu.VMEM((TOK, 8 * B), BF16),
            pltpu.VMEM((TOK, 8 * B), BF16),
            pltpu.VMEM((8, B, 4 * B), BF16),
            pltpu.VMEM((8, B, B), BF16),
            pltpu.VMEM((8, B, 4 * B), BF16),
            pltpu.VMEM((3, TOK, B), BF16),
            pltpu.VMEM((3, TOK, B), BF16),
            pltpu.VMEM((4, TOK, B), BF16),
            pltpu.VMEM((4, TOK, B), BF16),
            pltpu.VMEM((TOK, B), F32),
            pltpu.VMEM((TOK, B), F32),
            pltpu.VMEM((TOK, B), BF16),
            pltpu.VMEM((CHUNKS, 4, SUB, B), BF16),
            pltpu.VMEM((CHUNKS, B, B), F32),
            pltpu.VMEM((LENGTH, 3 * HEAD_DIM), BF16),
            pltpu.VMEM((TOK, 128), F32),
            pltpu.VMEM((TOK, HEAD_DIM), F32),
            pltpu.VMEM((TOK, HEAD_DIM), F32),
            pltpu.VMEM((4 * HB, HEAD_DIM), BF16),
            pltpu.VMEM((8, 1, TOK), F32),
            pltpu.VMEM((4, 1, TOK), F32),
            dma((6,)),
            dma((2, TURNS)),
            dma((2, TURNS)),
            dma((2, TURNS, 3, 2)),
            dma((2, TURNS, 8, 2)),
            dma((8,)),
            dma((8,)),
            dma((4,)),
            dma((4,)),
            dma((2, 8)),
            dma((2, 2, 4)),
            dma((2, 5)),
            dma((2, 5)),
            dma((3,)),
            dma((3,)),
            dma((2, TURNS, 4)),
            dma((2, TURNS, 4)),
            dma((CHUNKS, 4)),
            dma((CHUNKS, 4)),
            dma((CHUNKS, 8)),
            dma((2, CHUNKS, 4)),
            dma((2,)),
            dma((2,)),
        ],
        compiler_params=pltpu.CompilerParams(
            collective_id=0, has_side_effects=True, vmem_limit_bytes=58 * 2**20
        ),
    )(
        activations,
        norm_gain,
        w_query.reshape(2, 4, B, B),
        w_key.reshape(2, 4, B, 1024),
        w_value.reshape(2, 4, B, 1024),
        w_out.reshape(2, 4, B, B),
        cos,
        sin,
    )


def solution(mesh):
    placed = (
        P("row", "col"),
        P("col"),
        P("row", "col"),
        P("row", None),
        P("row", None),
        P("row", "col"),
    )
    return jax.shard_map(
        local_step, mesh=mesh, in_specs=placed, out_specs=P("row", "col"), check_vma=False
    )
```
